32 devices in a mesh: grp: 2 (over x), hor: 8 (over z, y), dep: 2 (over core).
Axes of the slice: x: 2, y: 2, z: 4, core: 2. Of those that a mesh axis runs over, the one named last changes fastest.
Arguments:
- residual: float32 [64, 64, 1024], P(('grp', 'dep'), 'hor'), parts along dimension 0, may hold values from -6 to 6
- focus_bins: int32 [64, 64, 1024], P(('grp', 'dep'), 'hor'), parts along dimension 0, may hold values from 0 to 15
- layer_class: int32 [64], P('grp'), parts along dimension 0, may hold values from 0 to 7
Outputs:
- preconditioned: float32 [64, 64, 1024], P(('grp', 'dep'), 'hor'), parts along dimension 0
The draws below stay inside these ranges and needn't reach their ends.
There are 2 independent parts, one for each index of `grp`. The reference program is written for one: setup_inputs(seed, part) draws one part's arguments, and reference() takes and returns one part's arrays. A program takes and returns all parts, laid end to end along the dimension named above; each array names one. Nothing has to cross between parts.
All inputs are finite; a program needn't handle non-finite values.
Results may differ from the reference program's by a relative error of at most 0.0003.
Values sent between devices are 32-bit elements; how exact they have to be, the bound alone decides.
A program may use at most 128 MiB of HBM per device.

```python
import math
import jax
import jax.numpy as jnp
from jax import lax

NZ = 32
NX = 1024
NY = 64
NCLASS = 8
NBINS = 16


def place_ends(drawn, stream_key, least, largest):
    spot = [jax.random.randint(jax.random.fold_in(stream_key, axis), (), 0, length) for axis, length in enumerate(drawn.shape)]
    main_axis = drawn.shape.index(max(drawn.shape))
    next_to = spot[:main_axis] + [(spot[main_axis] + 1) % drawn.shape[main_axis]] + spot[main_axis + 1:]
    return drawn.at[tuple(spot)].set(least).at[tuple(next_to)].set(largest)


def steps_of(key, dims, cuts, least, largest):
    gain, own = 1.0, jax.random.fold_in(key, 6)
    for axis_at, blocks in cuts:
        draws = jnp.exp(jax.random.uniform(jax.random.fold_in(own, axis_at), (blocks,), jnp.float32, least / len(cuts), largest / len(cuts)))
        gain = gain * jnp.repeat(draws, dims[axis_at] // blocks).reshape([-1 if axis == axis_at else 1 for axis in range(len(dims))])
    return gain


def bell_draw(rng, dims, width, reach, split=(), kind=jnp.bfloat16):
    factor_of = steps_of(rng, dims, split, -0.22, 0.18) if split else 1.0
    entries = jax.random.normal(rng, dims, jnp.float32) * width * factor_of
    return jnp.minimum(jnp.maximum(entries, -reach), reach).astype(kind)


def setup_inputs(seed: int = 0, part: int = 0) -> dict:
    streams_of = jax.random.split(jax.random.key(seed), 4)
    own_keys = jax.random.split(jax.random.fold_in(streams_of[3], part), 4)
    return {
        "residual": bell_draw(own_keys[0], (NZ, NY, NX), 1.0, 6.0, ((0, 2), (1, 8)), jnp.float32),
        "focus_bins": place_ends(jax.random.randint(own_keys[1], (NZ, NY, NX), 0, NBINS), jax.random.fold_in(own_keys[1], 1), 0, NBINS - 1).astype(jnp.int32),
        "layer_class": place_ends(jax.random.randint(own_keys[2], (NZ,), 0, NCLASS), jax.random.fold_in(own_keys[2], 1), 0, NCLASS - 1).astype(jnp.int32),
    }


damping = 0.01
smoothing = 1.0
coupling_scale = 1.0
weight_base = 0.5
weight_step = 0.2
focus_base = 0.5
focus_step = 0.09242


def depth_weights(layer_class):
    return weight_base * jnp.exp(weight_step * layer_class.astype(jnp.float32))


def focusing(focus_bins):
    return focus_base * jnp.exp(focus_step * focus_bins.astype(jnp.float32))


def couplings(weights):
    inner = coupling_scale * weights[:-1] * weights[1:]
    zero_end = jnp.zeros((1,), jnp.float32)
    return jnp.concatenate([zero_end, inner]), jnp.concatenate([inner, zero_end])


def symbol(frequency, length):
    return 2.0 - 2.0 * jnp.cos(frequency * (2.0 * math.pi / length))


def hartley(values, axis):
    spectrum = jnp.fft.fft(values, axis=axis)
    return jnp.real(spectrum) - jnp.imag(spectrum)


def reference(residual, focus_bins, layer_class):
    focus_map = focusing(focus_bins)
    scaled = focus_map * residual
    spectrum = hartley(hartley(scaled, 2), 1)
    weights = depth_weights(layer_class)
    couple_prev, couple_next = couplings(weights)
    symbol_x = symbol(jnp.arange(NX, dtype=jnp.float32), NX)
    symbol_y = symbol(jnp.arange(NY, dtype=jnp.float32), NY)
    wave_term = damping + smoothing * (symbol_y[:, None] + symbol_x[None, :])

    def forward(carried, inputs):
        prev_upper, prev_source = carried
        layer_plane, weight, lower, upper = inputs
        middle = weight * wave_term + (lower + upper)
        pivots = middle + lower * prev_upper
        now_upper = -upper / pivots
        now_source = (layer_plane + lower * prev_source) / pivots
        return (now_upper, now_source), (now_upper, now_source)

    zero_plane = jnp.zeros((NY, NX), jnp.float32)
    _, (uppers, sources) = lax.scan(forward, (zero_plane, zero_plane), (spectrum, weights, couple_prev, couple_next))

    def backward(following, inputs):
        upper, source = inputs
        result = source - upper * following
        return result, result

    _, solved = lax.scan(backward, zero_plane, (uppers, sources), reverse=True)
    restored = hartley(hartley(solved, 2), 1)
    return focus_map * restored / (NX * NY)
```

```python
import functools
import math

import jax
import jax.numpy as jnp
import ml_dtypes
import numpy as np
from jax import lax
from jax.experimental import pallas as pl
from jax.experimental.pallas import tpu as pltpu
from jax.sharding import PartitionSpec as P

damping = 0.01
smoothing = 1.0
coupling_scale = 1.0
weight_base = 0.5
weight_step = 0.2
focus_base = 0.5
focus_step = 0.09242
highest = lax.Precision.HIGHEST


def partner_2(value, axis, distance):
    mask = 2**distance
    pairs = [(source, source ^ mask) for source in range(lax.axis_size(axis))]
    return lax.ppermute(value, axis, pairs)


def depth_weights(layer_class):
    return weight_base * jnp.exp(weight_step * layer_class.astype(jnp.float32))


def focusing(focus_bins):
    return focus_base * jnp.exp(focus_step * focus_bins.astype(jnp.float32))


def couplings(weights):
    inner = coupling_scale * weights[:-1] * weights[1:]
    zero_end = jnp.zeros((1,), jnp.float32)
    return (jnp.concatenate([zero_end, inner]), jnp.concatenate([inner, zero_end]))


def symbol(frequency, length):
    return 2.0 - 2.0 * jnp.cos(frequency * (2.0 * math.pi / length))


def cas_table(length):
    position = jnp.arange(length, dtype=jnp.int32)
    product = position[:, None] * position[None, :] % length
    angles = product.astype(jnp.float32) * (2.0 * math.pi / length)
    return jnp.cos(angles) + jnp.sin(angles)


def shift_down(values, distance, fill_value):
    filler = jnp.full(values.shape[:-2] + (distance, values.shape[-1]), fill_value, values.dtype)
    return jnp.concatenate([filler, values[..., :-distance, :]], axis=-2)


def shift_up(values, distance, fill_value):
    filler = jnp.full(values.shape[:-2] + (distance, values.shape[-1]), fill_value, values.dtype)
    return jnp.concatenate([values[..., distance:, :], filler], axis=-2)


def reduce_step(lower, middle, upper, source, rows_below, rows_above):
    lower_below, middle_below, upper_below, source_below = rows_below
    lower_above, middle_above, upper_above, source_above = rows_above
    ratio_below = -lower / middle_below
    ratio_above = -upper / middle_above
    new_lower = ratio_below * lower_below
    new_middle = middle + ratio_below * upper_below + ratio_above * lower_above
    new_upper = ratio_above * upper_above
    new_source = source + ratio_below * source_below + ratio_above * source_above
    return (new_lower, new_middle, new_upper, new_source)


def local_solve(lower, middle, upper, source):
    layer_count = middle.shape[0]
    distance = 1
    while distance < layer_count:
        rows_below = (
            shift_down(lower, distance, 0.0),
            shift_down(middle, distance, 1.0),
            shift_down(upper, distance, 0.0),
            shift_down(source, distance, 0.0),
        )
        rows_above = (
            shift_up(lower, distance, 0.0),
            shift_up(middle, distance, 1.0),
            shift_up(upper, distance, 0.0),
            shift_up(source, distance, 0.0),
        )
        lower, middle, upper, source = reduce_step(
            lower, middle, upper, source, rows_below, rows_above
        )
        distance = distance * 2
    return source / middle


def body(residual, focus_bins, layer_class):
    depth_rows, y_rows, x_cells = residual.shape
    hor_count = lax.axis_size("hor")
    y_cells = y_rows * hor_count
    focus_map = focusing(focus_bins)
    scaled = focus_map * residual
    weights = depth_weights(layer_class)
    couple_prev, couple_next = couplings(weights)
    first_row = lax.axis_index("dep") * depth_rows
    table_x = cas_table(x_cells)
    table_y = cas_table(y_cells)
    symbol_y = symbol(jnp.arange(y_cells, dtype=jnp.float32), y_cells)
    block_width = x_cells // hor_count
    block_index = lax.axis_index("hor")
    spectra = jnp.einsum(
        "zcx,xbj->bzcj", scaled, table_x.reshape(x_cells, hor_count, block_width), precision=highest
    )
    spectra = spectra.reshape(hor_count, depth_rows, y_rows * block_width)
    table_rows = table_y.reshape(hor_count, y_rows, y_cells)
    portion = lax.all_to_all(spectra, "hor", split_axis=0, concat_axis=0, tiled=True)
    item_count = portion.shape[1]
    arranged = portion.reshape(hor_count, item_count, y_rows, block_width)
    spectrum = jnp.einsum("hzcj,hcy->zjy", arranged, table_rows, precision=highest)
    spectrum = spectrum.reshape(depth_rows, block_width * y_cells)
    wave_x = (block_index * block_width + jnp.arange(block_width, dtype=jnp.int32)).astype(
        jnp.float32
    )
    wave_term = (
        damping + smoothing * (symbol_y[None, :] + symbol(wave_x, x_cells)[:, None])
    ).reshape(-1)
    weight_local = lax.dynamic_slice_in_dim(weights, first_row, depth_rows)
    prev_local = lax.dynamic_slice_in_dim(couple_prev, first_row, depth_rows)
    next_local = lax.dynamic_slice_in_dim(couple_next, first_row, depth_rows)
    middle = weight_local[:, None] * wave_term[None, :] + (prev_local + next_local)[:, None]
    lower = jnp.broadcast_to(-prev_local[:, None], middle.shape)
    upper = jnp.broadcast_to(-next_local[:, None], middle.shape)
    row_index = jnp.arange(depth_rows, dtype=jnp.int32)
    edge_term = jnp.where(row_index == 0, prev_local[0], 0.0) + jnp.where(
        row_index == depth_rows - 1, next_local[depth_rows - 1], 0.0
    )
    source = jnp.stack([spectrum, jnp.broadcast_to(edge_term[:, None], spectrum.shape)])
    solutions = local_solve(lower, middle, upper, source)
    base_part = solutions[0]
    response = solutions[1]
    edge_row = (1 - lax.axis_index("dep")) * (depth_rows - 1)
    base_edge = lax.dynamic_index_in_dim(base_part, edge_row, 0, keepdims=False)
    response_edge = lax.dynamic_index_in_dim(response, edge_row, 0, keepdims=False)
    partner = partner_2(jnp.stack([base_edge, response_edge]), "dep", 0)
    divisor = 1.0 - response_edge * partner[1]
    interface = (partner[0] + partner[1] * base_edge) / divisor
    solved = base_part + response * interface[None, :]
    solved = solved.reshape(depth_rows, block_width, y_cells)
    returned = jnp.einsum(
        "zjk,khc->hzcj", solved, table_y.reshape(y_cells, hor_count, y_rows), precision=highest
    )
    returned = returned.reshape(hor_count, depth_rows, y_rows * block_width)
    table_back = table_x.reshape(hor_count, block_width, x_cells)
    portion = lax.all_to_all(returned, "hor", split_axis=0, concat_axis=0, tiled=True)
    item_count = portion.shape[1]
    arranged = portion.reshape(hor_count, item_count, y_rows, block_width)
    result_field = jnp.einsum("bzcj,bjx->zcx", arranged, table_back, precision=highest)
    return focus_map * result_field / (x_cells * y_cells)

MESH = pl.DeviceIdType.MESH
GROUP = 4


def split_table(length):
    position = np.arange(length)
    angles = (position[:, None] * position[None, :] % length) * (2.0 * math.pi / length)
    table = np.cos(angles) + np.sin(angles)
    high = table.astype(ml_dtypes.bfloat16)
    low = (table - high.astype(np.float64)).astype(ml_dtypes.bfloat16)
    return high, low


def split_values(values):
    high = values.astype(jnp.bfloat16)
    low = (values - high.astype(jnp.float32)).astype(jnp.bfloat16)
    return high, low


def dot32(left, right):
    return jnp.dot(left, right, preferred_element_type=jnp.float32)


def pair_order(mine):
    beside = mine + 1 - 2 * lax.rem(mine, 2)
    return [lax.rem(mine + 2, 4), 3 - mine, beside, mine]


def kernel(
    residual,
    bins,
    classes,
    table_high,
    table_low,
    table_y,
    wave_x,
    wave_y,
    field,
    res_v,
    bins_v,
    high_v,
    low_v,
    send_a,
    recv_a,
    send_b,
    recv_b,
    weights,
    spectrum,
    inverse,
    factor,
    edge_out,
    edge_in,
    load_sem,
    high_sem,
    low_sem,
    send_a_sem,
    recv_a_sem,
    send_b_sem,
    recv_b_sem,
    edge_send_sem,
    edge_recv_sem,
):
    count, layers, y_rows, width = send_a.shape
    y_cells = count * y_rows
    rows = layers * y_rows
    me = lax.axis_index("hor")
    half = lax.axis_index("dep")
    order = pair_order(me // 2)

    loads = [
        pltpu.make_async_copy(residual, res_v, load_sem.at[0]),
        pltpu.make_async_copy(bins, bins_v, load_sem.at[1]),
    ]
    for load in loads:
        load.start()
    table_loads = []
    for pair in order:
        both = [
            pltpu.make_async_copy(table_high.at[pair], high_v.at[pair], high_sem.at[pair]),
            pltpu.make_async_copy(table_low.at[pair], low_v.at[pair], low_sem.at[pair]),
        ]
        for load in both:
            load.start()
        table_loads.append(both)

    barrier = pltpu.get_barrier_semaphore()
    for step in range(1, count):
        pl.semaphore_signal(
            barrier, inc=1, device_id={"hor": lax.rem(me + step, count)}, device_id_type=MESH
        )
    pl.semaphore_signal(barrier, inc=1, device_id={"dep": 1 - half}, device_id_type=MESH)

    for load in loads:
        load.wait()
    focus_map = focus_base * jnp.exp(focus_step * bins_v[...].astype(jnp.float32))
    scaled = (focus_map * res_v[...]).reshape(rows, count * width)
    high, low = split_values(scaled)
    stacked = jnp.concatenate([high, low], axis=0)

    def send_forward(target):
        return pltpu.make_async_remote_copy(
            src_ref=send_a.at[target],
            dst_ref=recv_a.at[me],
            send_sem=send_a_sem.at[target],
            recv_sem=recv_a_sem.at[me],
            device_id={"hor": target},
            device_id_type=MESH,
        )

    other = me + 1 - 2 * lax.rem(me, 2)
    for step, pair in enumerate(order):
        for load in table_loads[step]:
            load.wait()
        first = dot32(stacked, high_v[pair])
        value = first[:rows] + first[rows:] + dot32(high, low_v[pair])
        send_a[2 * pair] = value[:, :width].reshape(layers, y_rows, width)
        send_a[2 * pair + 1] = value[:, width:].reshape(layers, y_rows, width)
        if step == 0:
            pl.semaphore_wait(barrier, count)
        if step < 3:
            send_forward(2 * pair).start()
            send_forward(2 * pair + 1).start()
        else:
            send_forward(other).start()
    recv_a[me] = send_a[me]

    for layer in range(2 * layers):
        index = jnp.full((8, width), classes[0, layer], jnp.int32).astype(jnp.float32)
        weights[layer] = weight_base * jnp.exp(weight_step * index)

    def layer_of(place):
        return place + half * (layers - 1 - 2 * place)

    def coupling_after(place):
        here = half * layers + layer_of(place)
        return coupling_scale * weights[here] * weights[here + 1 - 2 * half]

    wave = (damping + smoothing * (wave_y[...] + wave_x[me][None])).reshape(y_cells // 8, 8, width)

    def pivot_step(place, carried):
        excess_part = carried
        here = weights[half * layers + layer_of(place)]
        excess = here[None] * wave + excess_part
        after = coupling_after(place)[None]
        reciprocal = 1.0 / (excess + after)
        inverse[place] = reciprocal
        scaled_after = after * reciprocal
        factor[place] = scaled_after
        edge_out[0] = excess
        return scaled_after * excess

    lax.fori_loop(0, layers, pivot_step, jnp.zeros_like(wave))

    def edge_copy(slot):
        return pltpu.make_async_remote_copy(
            src_ref=edge_out.at[slot],
            dst_ref=edge_in.at[slot],
            send_sem=edge_send_sem.at[slot],
            recv_sem=edge_recv_sem.at[slot],
            device_id={"dep": 1 - half},
            device_id_type=MESH,
        )

    edge_copy(0).start()

    for step in range(1, count):
        source = lax.rem(me + step, count)
        pltpu.make_async_remote_copy(
            src_ref=send_a.at[source],
            dst_ref=recv_a.at[source],
            send_sem=send_a_sem.at[source],
            recv_sem=recv_a_sem.at[source],
            device_id={"hor": source},
            device_id_type=MESH,
        ).wait_recv()

    def transform_y(first, second):
        values = jnp.concatenate([first, second], axis=1)
        upper, lower = split_values(values)
        return dot32(table_y[...], jnp.concatenate([upper, upper, lower], axis=0))

    def spectrum_step(index, carried):
        first = recv_a[:, 2 * index].reshape(y_cells, width)
        second = recv_a[:, 2 * index + 1].reshape(y_cells, width)
        value = transform_y(first, second)
        spectrum[2 * index] = value[:, :width].reshape(y_cells // 8, 8, width)
        spectrum[2 * index + 1] = value[:, width:].reshape(y_cells // 8, 8, width)
        return carried

    lax.fori_loop(0, layers // 2, spectrum_step, 0)

    def forward_step(place, carried):
        here = spectrum[layer_of(place)] + carried
        spectrum[layer_of(place)] = here
        return factor[place] * here

    lax.fori_loop(0, layers - 1, forward_step, jnp.zeros_like(wave))
    edge_out[1] = spectrum[layer_of(layers - 1)] + factor[layers - 2] * spectrum[layer_of(layers - 2)]
    edge_copy(1).start()
    edge_copy(0).wait()
    excess_here = edge_out[0]
    excess_there = edge_in[0]
    after = coupling_after(layers - 1)[None]
    scale = 1.0 / (excess_here * excess_there + after * (excess_here + excess_there))
    edge_copy(1).wait()
    last = ((excess_there + after) * edge_out[1] + after * edge_in[1]) * scale
    spectrum[layer_of(layers - 1)] = last

    def send_back(group, target):
        start = group * GROUP + half * (layers - GROUP - 2 * group * GROUP)
        return pltpu.make_async_remote_copy(
            src_ref=send_b.at[target, pl.ds(start, GROUP)],
            dst_ref=recv_b.at[me, pl.ds(start, GROUP)],
            send_sem=send_b_sem.at[group, target],
            recv_sem=recv_b_sem.at[group, me],
            device_id={"hor": target},
            device_id_type=MESH,
        )

    def wait_back(group, source):
        start = group * GROUP + half * (layers - GROUP - 2 * group * GROUP)
        pltpu.make_async_remote_copy(
            src_ref=send_b.at[source, pl.ds(start, GROUP)],
            dst_ref=recv_b.at[source, pl.ds(start, GROUP)],
            send_sem=send_b_sem.at[group, source],
            recv_sem=recv_b_sem.at[group, source],
            device_id={"hor": source},
            device_id_type=MESH,
        ).wait_recv()

    def backward_step(place, following):
        here = layer_of(place)
        value = inverse[place] * spectrum[here] + factor[place] * following
        spectrum[here] = value
        return value

    following = last
    groups = layers // GROUP
    for group in reversed(range(groups)):
        for place in reversed(range(group * GROUP, (group + 1) * GROUP)):
            if place < layers - 1:
                following = backward_step(place, following)
        for place in range(group * GROUP, (group + 1) * GROUP, 2):
            first = layer_of(place)
            second = layer_of(place + 1)
            value = transform_y(
                spectrum[first].reshape(y_cells, width), spectrum[second].reshape(y_cells, width)
            )
            send_b[:, first] = value[:, :width].reshape(count, y_rows, width)
            send_b[:, second] = value[:, width:].reshape(count, y_rows, width)
        for pair in order[:3]:
            send_back(group, 2 * pair).start()
            send_back(group, 2 * pair + 1).start()
        send_back(group, other).start()
    recv_b[me] = send_b[me]

    for step, pair in enumerate(reversed(order)):
        for group in reversed(range(groups)):
            if step > 0:
                wait_back(group, 2 * pair)
                wait_back(group, 2 * pair + 1)
            else:
                wait_back(group, other)
        value = jnp.concatenate(
            [recv_b[2 * pair].reshape(rows, width), recv_b[2 * pair + 1].reshape(rows, width)],
            axis=1,
        )
        upper, lower = split_values(value)
        stacked = jnp.concatenate([upper, lower], axis=0)
        start = pl.multiple_of(pair * 2 * width, 2 * width)
        for block in range(count // 2):
            first = dot32(stacked, high_v[block, pl.ds(start, 2 * width)])
            total = first[:rows] + first[rows:] + dot32(upper, low_v[block, pl.ds(start, 2 * width)])
            columns = slice(block * 2 * width, (block + 1) * 2 * width)
            total = total.reshape(layers, y_rows, 2 * width)
            if step > 0:
                total = total + field[:, :, columns]
            field[:, :, columns] = total

    for step in range(1, count):
        target = lax.rem(me + step, count)
        send_forward(target).wait_send()
        for group in range(groups):
            send_back(group, target).wait_send()


def kernel_body(residual, focus_bins, layer_class):
    layers, y_rows, x_cells = residual.shape
    count = lax.axis_size("hor")
    width = x_cells // count
    y_cells = y_rows * count
    high, low = split_table(x_cells)
    high = np.ascontiguousarray(high.reshape(x_cells, count // 2, 2 * width).transpose(1, 0, 2))
    low = np.ascontiguousarray(low.reshape(x_cells, count // 2, 2 * width).transpose(1, 0, 2))
    high_y, low_y = split_table(y_cells)
    table_y = np.concatenate([high_y, low_y, high_y], axis=1)
    wave_x = 2.0 - 2.0 * np.cos(np.arange(x_cells) * (2.0 * math.pi / x_cells))
    wave_x = np.broadcast_to(wave_x.reshape(count, 1, width), (count, 8, width))
    wave_x = np.tile(wave_x, (1, y_cells // 8, 1)).astype(np.float32)
    wave_y = 2.0 - 2.0 * np.cos(np.arange(y_cells) * (2.0 * math.pi / y_cells))
    wave_y = np.broadcast_to(wave_y[:, None], (y_cells, width)).astype(np.float32)
    block = (count, layers, y_rows, width)
    column = (layers, y_cells // 8, 8, width)
    f32, dma = jnp.float32, pltpu.SemaphoreType.DMA
    hbm = pl.BlockSpec(memory_space=pl.ANY)
    vmem = pl.BlockSpec(memory_space=pltpu.VMEM)
    smem = pl.BlockSpec(memory_space=pltpu.SMEM)
    field = pl.pallas_call(
        kernel,
        out_shape=jax.ShapeDtypeStruct(residual.shape, f32),
        in_specs=[hbm, hbm, smem, hbm, hbm, vmem, vmem, vmem],
        out_specs=vmem,
        scratch_shapes=[
            pltpu.VMEM(residual.shape, f32),
            pltpu.VMEM(residual.shape, jnp.int32),
            pltpu.VMEM(high.shape, jnp.bfloat16),
            pltpu.VMEM(low.shape, jnp.bfloat16),
            pltpu.VMEM(block, f32),
            pltpu.VMEM(block, f32),
            pltpu.VMEM(block, f32),
            pltpu.VMEM(block, f32),
            pltpu.VMEM((2 * layers, 8, width), f32),
            pltpu.VMEM(column, f32),
            pltpu.VMEM(column, f32),
            pltpu.VMEM(column, f32),
            pltpu.VMEM((2,) + column[1:], f32),
            pltpu.VMEM((2,) + column[1:], f32),
            dma((2,)),
            dma((count // 2,)),
            dma((count // 2,)),
            dma((count,)),
            dma((count,)),
            dma((layers // GROUP, count)),
            dma((layers // GROUP, count)),
            dma((2,)),
            dma((2,)),
        ],
        compiler_params=pltpu.CompilerParams(
            collective_id=0, has_side_effects=True, vmem_limit_bytes=40 * 2**20
        ),
        cost_estimate=pl.CostEstimate(
            flops=2 * 6 * layers * y_rows * x_cells * x_cells,
            bytes_accessed=6 * 2**20,
            transcendentals=layers * y_rows * x_cells,
        ),
    )(
        residual,
        focus_bins,
        layer_class.reshape(1, -1),
        jnp.asarray(high),
        jnp.asarray(low),
        jnp.asarray(table_y),
        jnp.asarray(wave_x),
        jnp.asarray(wave_y),
    )
    return focusing(focus_bins) * field * (1.0 / (x_cells * y_cells))


def fits_kernel(mesh):
    return mesh.shape["hor"] == 8 and mesh.shape["dep"] == 2


def chosen(mesh, residual, focus_bins, layer_class):
    shape = residual.shape
    if fits_kernel(mesh) and shape[1] % 8 == 0 and shape[2] == 1024 and shape[0] % GROUP == 0:
        return kernel_body(residual, focus_bins, layer_class)
    return body(residual, focus_bins, layer_class)


def solution(mesh):
    return jax.shard_map(
        functools.partial(chosen, mesh),
        mesh=mesh,
        in_specs=(P(("grp", "dep"), "hor", None), P(("grp", "dep"), "hor", None), P("grp")),
        out_specs=P(("grp", "dep"), "hor", None),
        check_vma=False,
    )
```

```python
import functools
import math

import jax
import jax.numpy as jnp
import ml_dtypes
import numpy as np
from jax import lax
from jax.experimental import pallas as pl
from jax.experimental.pallas import tpu as pltpu
from jax.sharding import PartitionSpec as P

damping = 0.01
smoothing = 1.0
coupling_scale = 1.0
weight_base = 0.5
weight_step = 0.2
focus_base = 0.5
focus_step = 0.09242
highest = lax.Precision.HIGHEST


def partner_2(value, axis, distance):
    mask = 2**distance
    pairs = [(source, source ^ mask) for source in range(lax.axis_size(axis))]
    return lax.ppermute(value, axis, pairs)


def depth_weights(layer_class):
    return weight_base * jnp.exp(weight_step * layer_class.astype(jnp.float32))


def focusing(focus_bins):
    return focus_base * jnp.exp(focus_step * focus_bins.astype(jnp.float32))


def couplings(weights):
    inner = coupling_scale * weights[:-1] * weights[1:]
    zero_end = jnp.zeros((1,), jnp.float32)
    return (jnp.concatenate([zero_end, inner]), jnp.concatenate([inner, zero_end]))


def symbol(frequency, length):
    return 2.0 - 2.0 * jnp.cos(frequency * (2.0 * math.pi / length))


def cas_table(length):
    position = jnp.arange(length, dtype=jnp.int32)
    product = position[:, None] * position[None, :] % length
    angles = product.astype(jnp.float32) * (2.0 * math.pi / length)
    return jnp.cos(angles) + jnp.sin(angles)


def shift_down(values, distance, fill_value):
    filler = jnp.full(values.shape[:-2] + (distance, values.shape[-1]), fill_value, values.dtype)
    return jnp.concatenate([filler, values[..., :-distance, :]], axis=-2)


def shift_up(values, distance, fill_value):
    filler = jnp.full(values.shape[:-2] + (distance, values.shape[-1]), fill_value, values.dtype)
    return jnp.concatenate([values[..., distance:, :], filler], axis=-2)


def reduce_step(lower, middle, upper, source, rows_below, rows_above):
    lower_below, middle_below, upper_below, source_below = rows_below
    lower_above, middle_above, upper_above, source_above = rows_above
    ratio_below = -lower / middle_below
    ratio_above = -upper / middle_above
    new_lower = ratio_below * lower_below
    new_middle = middle + ratio_below * upper_below + ratio_above * lower_above
    new_upper = ratio_above * upper_above
    new_source = source + ratio_below * source_below + ratio_above * source_above
    return (new_lower, new_middle, new_upper, new_source)


def local_solve(lower, middle, upper, source):
    layer_count = middle.shape[0]
    distance = 1
    while distance < layer_count:
        rows_below = (
            shift_down(lower, distance, 0.0),
            shift_down(middle, distance, 1.0),
            shift_down(upper, distance, 0.0),
            shift_down(source, distance, 0.0),
        )
        rows_above = (
            shift_up(lower, distance, 0.0),
            shift_up(middle, distance, 1.0),
            shift_up(upper, distance, 0.0),
            shift_up(source, distance, 0.0),
        )
        lower, middle, upper, source = reduce_step(
            lower, middle, upper, source, rows_below, rows_above
        )
        distance = distance * 2
    return source / middle


def body(residual, focus_bins, layer_class):
    depth_rows, y_rows, x_cells = residual.shape
    hor_count = lax.axis_size("hor")
    y_cells = y_rows * hor_count
    focus_map = focusing(focus_bins)
    scaled = focus_map * residual
    weights = depth_weights(layer_class)
    couple_prev, couple_next = couplings(weights)
    first_row = lax.axis_index("dep") * depth_rows
    table_x = cas_table(x_cells)
    table_y = cas_table(y_cells)
    symbol_y = symbol(jnp.arange(y_cells, dtype=jnp.float32), y_cells)
    block_width = x_cells // hor_count
    block_index = lax.axis_index("hor")
    spectra = jnp.einsum(
        "zcx,xbj->bzcj", scaled, table_x.reshape(x_cells, hor_count, block_width), precision=highest
    )
    spectra = spectra.reshape(hor_count, depth_rows, y_rows * block_width)
    table_rows = table_y.reshape(hor_count, y_rows, y_cells)
    portion = lax.all_to_all(spectra, "hor", split_axis=0, concat_axis=0, tiled=True)
    item_count = portion.shape[1]
    arranged = portion.reshape(hor_count, item_count, y_rows, block_width)
    spectrum = jnp.einsum("hzcj,hcy->zjy", arranged, table_rows, precision=highest)
    spectrum = spectrum.reshape(depth_rows, block_width * y_cells)
    wave_x = (block_index * block_width + jnp.arange(block_width, dtype=jnp.int32)).astype(
        jnp.float32
    )
    wave_term = (
        damping + smoothing * (symbol_y[None, :] + symbol(wave_x, x_cells)[:, None])
    ).reshape(-1)
    weight_local = lax.dynamic_slice_in_dim(weights, first_row, depth_rows)
    prev_local = lax.dynamic_slice_in_dim(couple_prev, first_row, depth_rows)
    next_local = lax.dynamic_slice_in_dim(couple_next, first_row, depth_rows)
    middle = weight_local[:, None] * wave_term[None, :] + (prev_local + next_local)[:, None]
    lower = jnp.broadcast_to(-prev_local[:, None], middle.shape)
    upper = jnp.broadcast_to(-next_local[:, None], middle.shape)
    row_index = jnp.arange(depth_rows, dtype=jnp.int32)
    edge_term = jnp.where(row_index == 0, prev_local[0], 0.0) + jnp.where(
        row_index == depth_rows - 1, next_local[depth_rows - 1], 0.0
    )
    source = jnp.stack([spectrum, jnp.broadcast_to(edge_term[:, None], spectrum.shape)])
    solutions = local_solve(lower, middle, upper, source)
    base_part = solutions[0]
    response = solutions[1]
    edge_row = (1 - lax.axis_index("dep")) * (depth_rows - 1)
    base_edge = lax.dynamic_index_in_dim(base_part, edge_row, 0, keepdims=False)
    response_edge = lax.dynamic_index_in_dim(response, edge_row, 0, keepdims=False)
    partner = partner_2(jnp.stack([base_edge, response_edge]), "dep", 0)
    divisor = 1.0 - response_edge * partner[1]
    interface = (partner[0] + partner[1] * base_edge) / divisor
    solved = base_part + response * interface[None, :]
    solved = solved.reshape(depth_rows, block_width, y_cells)
    returned = jnp.einsum(
        "zjk,khc->hzcj", solved, table_y.reshape(y_cells, hor_count, y_rows), precision=highest
    )
    returned = returned.reshape(hor_count, depth_rows, y_rows * block_width)
    table_back = table_x.reshape(hor_count, block_width, x_cells)
    portion = lax.all_to_all(returned, "hor", split_axis=0, concat_axis=0, tiled=True)
    item_count = portion.shape[1]
    arranged = portion.reshape(hor_count, item_count, y_rows, block_width)
    result_field = jnp.einsum("bzcj,bjx->zcx", arranged, table_back, precision=highest)
    return focus_map * result_field / (x_cells * y_cells)

MESH = pl.DeviceIdType.MESH
GROUP = 4


def split_table(length):
    position = np.arange(length)
    angles = (position[:, None] * position[None, :] % length) * (2.0 * math.pi / length)
    table = np.cos(angles) + np.sin(angles)
    high = table.astype(ml_dtypes.bfloat16)
    low = (table - high.astype(np.float64)).astype(ml_dtypes.bfloat16)
    return high, low


def split_values(values):
    high = values.astype(jnp.bfloat16)
    low = (values - high.astype(jnp.float32)).astype(jnp.bfloat16)
    return high, low


def dot32(left, right):
    return jnp.dot(left, right, preferred_element_type=jnp.float32)


def pair_order(mine):
    beside = mine + 1 - 2 * lax.rem(mine, 2)
    return [lax.rem(mine + 2, 4), 3 - mine, beside, mine]


def kernel(
    residual,
    bins,
    classes,
    table_high,
    table_low,
    table_y,
    wave_x,
    wave_y,
    field,
    res_v,
    bins_v,
    classes_v,
    table_y_v,
    wave_x_v,
    wave_y_v,
    high_v,
    low_v,
    send_a,
    recv_a,
    send_b,
    recv_b,
    weights,
    spectrum,
    inverse,
    factor,
    edge_out,
    edge_in,
    load_sem,
    high_sem,
    low_sem,
    send_a_sem,
    recv_a_sem,
    send_b_sem,
    recv_b_sem,
    edge_send_sem,
    edge_recv_sem,
):
    count, layers, y_rows, width = send_a.shape
    y_cells = count * y_rows
    rows = layers * y_rows
    me = lax.axis_index("hor")
    half = lax.axis_index("dep")
    order = pair_order(me // 2)

    barrier = pltpu.get_barrier_semaphore()
    for step in range(1, count):
        pl.semaphore_signal(
            barrier, inc=1, device_id={"hor": lax.rem(me + step, count)}, device_id_type=MESH
        )
    pl.semaphore_signal(barrier, inc=1, device_id={"dep": 1 - half}, device_id_type=MESH)

    loads = [
        pltpu.make_async_copy(residual, res_v, load_sem.at[0]),
        pltpu.make_async_copy(bins, bins_v, load_sem.at[1]),
    ]
    for load in loads:
        load.start()
    table_loads = []
    for pair in order:
        both = [
            pltpu.make_async_copy(table_high.at[pair], high_v.at[pair], high_sem.at[pair]),
            pltpu.make_async_copy(table_low.at[pair], low_v.at[pair], low_sem.at[pair]),
        ]
        for load in both:
            load.start()
        table_loads.append(both)
    late_loads = [
        pltpu.make_async_copy(classes, classes_v, load_sem.at[2]),
        pltpu.make_async_copy(table_y, table_y_v, load_sem.at[3]),
        pltpu.make_async_copy(wave_x.at[me], wave_x_v, load_sem.at[4]),
        pltpu.make_async_copy(wave_y, wave_y_v, load_sem.at[5]),
    ]
    for load in late_loads:
        load.start()

    for load in loads:
        load.wait()
    focus_map = focus_base * jnp.exp(focus_step * bins_v[...].astype(jnp.float32))
    scaled = (focus_map * res_v[...]).reshape(rows, count * width)
    high, low = split_values(scaled)
    stacked = jnp.concatenate([high, low], axis=0)

    def send_forward(target):
        return pltpu.make_async_remote_copy(
            src_ref=send_a.at[target],
            dst_ref=recv_a.at[me],
            send_sem=send_a_sem.at[target],
            recv_sem=recv_a_sem.at[me],
            device_id={"hor": target},
            device_id_type=MESH,
        )

    other = me + 1 - 2 * lax.rem(me, 2)
    for step, pair in enumerate(order):
        for load in table_loads[step]:
            load.wait()
        first = dot32(stacked, high_v[pair])
        value = first[:rows] + first[rows:] + dot32(high, low_v[pair])
        send_a[2 * pair] = value[:, :width].reshape(layers, y_rows, width)
        send_a[2 * pair + 1] = value[:, width:].reshape(layers, y_rows, width)
        if step == 0:
            pl.semaphore_wait(barrier, count)
        if step < 3:
            send_forward(2 * pair).start()
            send_forward(2 * pair + 1).start()
        else:
            send_forward(other).start()
    recv_a[me] = send_a[me]

    for load in late_loads:
        load.wait()
    for layer in range(2 * layers):
        index = jnp.full((8, width), classes_v[0, layer], jnp.int32).astype(jnp.float32)
        weights[layer] = weight_base * jnp.exp(weight_step * index)

    def layer_of(place):
        return place + half * (layers - 1 - 2 * place)

    def coupling_after(place):
        here = half * layers + layer_of(place)
        return coupling_scale * weights[here] * weights[here + 1 - 2 * half]

    wave = (damping + smoothing * (wave_y_v[...] + wave_x_v[...][None]))

    def pivot_step(place, carried):
        excess_part = carried
        here = weights[half * layers + layer_of(place)]
        excess = here[None] * wave + excess_part
        after = coupling_after(place)[None]
        reciprocal = 1.0 / (excess + after)
        inverse[place] = reciprocal
        scaled_after = after * reciprocal
        factor[place] = scaled_after
        edge_out[0] = excess
        return scaled_after * excess

    lax.fori_loop(0, layers, pivot_step, jnp.zeros_like(wave))

    def edge_copy(slot):
        return pltpu.make_async_remote_copy(
            src_ref=edge_out.at[slot],
            dst_ref=edge_in.at[slot],
            send_sem=edge_send_sem.at[slot],
            recv_sem=edge_recv_sem.at[slot],
            device_id={"dep": 1 - half},
            device_id_type=MESH,
        )

    edge_copy(0).start()

    for step in range(1, count):
        source = lax.rem(me + step, count)
        pltpu.make_async_remote_copy(
            src_ref=send_a.at[source],
            dst_ref=recv_a.at[source],
            send_sem=send_a_sem.at[source],
            recv_sem=recv_a_sem.at[source],
            device_id={"hor": source},
            device_id_type=MESH,
        ).wait_recv()

    def transform_y(first, second):
        values = jnp.concatenate([first, second], axis=1)
        upper, lower = split_values(values)
        return dot32(table_y_v[...], jnp.concatenate([upper, upper, lower], axis=0))

    def spectrum_step(index, carried):
        first = recv_a[:, 2 * index].reshape(y_cells, width)
        second = recv_a[:, 2 * index + 1].reshape(y_cells, width)
        value = transform_y(first, second)
        spectrum[2 * index] = value[:, :width].reshape(y_cells // 8, 8, width)
        spectrum[2 * index + 1] = value[:, width:].reshape(y_cells // 8, 8, width)
        return carried

    lax.fori_loop(0, layers // 2, spectrum_step, 0)

    def forward_step(place, carried):
        here = spectrum[layer_of(place)] + carried
        spectrum[layer_of(place)] = here
        return factor[place] * here

    lax.fori_loop(0, layers - 1, forward_step, jnp.zeros_like(wave))
    edge_out[1] = spectrum[layer_of(layers - 1)] + factor[layers - 2] * spectrum[layer_of(layers - 2)]
    edge_copy(1).start()
    edge_copy(0).wait()
    excess_here = edge_out[0]
    excess_there = edge_in[0]
    after = coupling_after(layers - 1)[None]
    scale = 1.0 / (excess_here * excess_there + after * (excess_here + excess_there))
    edge_copy(1).wait()
    last = ((excess_there + after) * edge_out[1] + after * edge_in[1]) * scale
    spectrum[layer_of(layers - 1)] = last

    def send_back(group, target):
        start = group * GROUP + half * (layers - GROUP - 2 * group * GROUP)
        return pltpu.make_async_remote_copy(
            src_ref=send_b.at[target, pl.ds(start, GROUP)],
            dst_ref=recv_b.at[me, pl.ds(start, GROUP)],
            send_sem=send_b_sem.at[group, target],
            recv_sem=recv_b_sem.at[group, me],
            device_id={"hor": target},
            device_id_type=MESH,
        )

    def wait_back(group, source):
        start = group * GROUP + half * (layers - GROUP - 2 * group * GROUP)
        pltpu.make_async_remote_copy(
            src_ref=send_b.at[source, pl.ds(start, GROUP)],
            dst_ref=recv_b.at[source, pl.ds(start, GROUP)],
            send_sem=send_b_sem.at[group, source],
            recv_sem=recv_b_sem.at[group, source],
            device_id={"hor": source},
            device_id_type=MESH,
        ).wait_recv()

    def backward_step(place, following):
        here = layer_of(place)
        value = inverse[place] * spectrum[here] + factor[place] * following
        spectrum[here] = value
        return value

    following = last
    groups = layers // GROUP
    for group in reversed(range(groups)):
        for place in reversed(range(group * GROUP, (group + 1) * GROUP)):
            if place < layers - 1:
                following = backward_step(place, following)
        for place in range(group * GROUP, (group + 1) * GROUP, 2):
            first = layer_of(place)
            second = layer_of(place + 1)
            value = transform_y(
                spectrum[first].reshape(y_cells, width), spectrum[second].reshape(y_cells, width)
            )
            send_b[:, first] = value[:, :width].reshape(count, y_rows, width)
            send_b[:, second] = value[:, width:].reshape(count, y_rows, width)
        for pair in order[:3]:
            send_back(group, 2 * pair).start()
            send_back(group, 2 * pair + 1).start()
        send_back(group, other).start()
    recv_b[me] = send_b[me]

    for step, pair in enumerate(reversed(order)):
        for group in reversed(range(groups)):
            if step > 0:
                wait_back(group, 2 * pair)
                wait_back(group, 2 * pair + 1)
            else:
                wait_back(group, other)
        value = jnp.concatenate(
            [recv_b[2 * pair].reshape(rows, width), recv_b[2 * pair + 1].reshape(rows, width)],
            axis=1,
        )
        upper, lower = split_values(value)
        stacked = jnp.concatenate([upper, lower], axis=0)
        start = pl.multiple_of(pair * 2 * width, 2 * width)
        for block in range(count // 2):
            first = dot32(stacked, high_v[block, pl.ds(start, 2 * width)])
            total = first[:rows] + first[rows:] + dot32(upper, low_v[block, pl.ds(start, 2 * width)])
            columns = slice(block * 2 * width, (block + 1) * 2 * width)
            total = total.reshape(layers, y_rows, 2 * width)
            if step > 0:
                total = total + field[:, :, columns]
            field[:, :, columns] = total

    for step in range(1, count):
        target = lax.rem(me + step, count)
        send_forward(target).wait_send()
        for group in range(groups):
            send_back(group, target).wait_send()


def kernel_body(residual, focus_bins, layer_class):
    layers, y_rows, x_cells = residual.shape
    count = lax.axis_size("hor")
    width = x_cells // count
    y_cells = y_rows * count
    high, low = split_table(x_cells)
    high = np.ascontiguousarray(high.reshape(x_cells, count // 2, 2 * width).transpose(1, 0, 2))
    low = np.ascontiguousarray(low.reshape(x_cells, count // 2, 2 * width).transpose(1, 0, 2))
    high_y, low_y = split_table(y_cells)
    table_y = np.concatenate([high_y, low_y, high_y], axis=1)
    wave_x = 2.0 - 2.0 * np.cos(np.arange(x_cells) * (2.0 * math.pi / x_cells))
    wave_x = np.broadcast_to(wave_x.reshape(count, 1, width), (count, 8, width)).astype(np.float32)
    wave_y = 2.0 - 2.0 * np.cos(np.arange(y_cells) * (2.0 * math.pi / y_cells))
    wave_y = np.broadcast_to(wave_y[:, None], (y_cells, width)).astype(np.float32)
    wave_y = wave_y.reshape(y_cells // 8, 8, width)
    block = (count, layers, y_rows, width)
    column = (layers, y_cells // 8, 8, width)
    f32, dma = jnp.float32, pltpu.SemaphoreType.DMA
    hbm = pl.BlockSpec(memory_space=pl.ANY)
    vmem = pl.BlockSpec(memory_space=pltpu.VMEM)
    field = pl.pallas_call(
        kernel,
        out_shape=jax.ShapeDtypeStruct(residual.shape, f32),
        in_specs=[hbm] * 8,
        out_specs=vmem,
        scratch_shapes=[
            pltpu.VMEM(residual.shape, f32),
            pltpu.VMEM(residual.shape, jnp.int32),
            pltpu.SMEM((1, 2 * layers), jnp.int32),
            pltpu.VMEM(table_y.shape, jnp.bfloat16),
            pltpu.VMEM((8, width), f32),
            pltpu.VMEM((y_cells // 8, 8, width), f32),
            pltpu.VMEM(high.shape, jnp.bfloat16),
            pltpu.VMEM(low.shape, jnp.bfloat16),
            pltpu.VMEM(block, f32),
            pltpu.VMEM(block, f32),
            pltpu.VMEM(block, f32),
            pltpu.VMEM(block, f32),
            pltpu.VMEM((2 * layers, 8, width), f32),
            pltpu.VMEM(column, f32),
            pltpu.VMEM(column, f32),
            pltpu.VMEM(column, f32),
            pltpu.VMEM((2,) + column[1:], f32),
            pltpu.VMEM((2,) + column[1:], f32),
            dma((6,)),
            dma((count // 2,)),
            dma((count // 2,)),
            dma((count,)),
            dma((count,)),
            dma((layers // GROUP, count)),
            dma((layers // GROUP, count)),
            dma((2,)),
            dma((2,)),
        ],
        compiler_params=pltpu.CompilerParams(
            collective_id=0, has_side_effects=True, vmem_limit_bytes=64 * 2**20
        ),
        cost_estimate=pl.CostEstimate(
            flops=2 * 6 * layers * y_rows * x_cells * x_cells,
            bytes_accessed=6 * 2**20,
            transcendentals=layers * y_rows * x_cells,
        ),
    )(
        residual,
        focus_bins,
        layer_class.reshape(1, -1),
        jnp.asarray(high),
        jnp.asarray(low),
        jnp.asarray(table_y),
        jnp.asarray(wave_x),
        jnp.asarray(wave_y),
    )
    return focusing(focus_bins) * field * (1.0 / (x_cells * y_cells))


def fits_kernel(mesh):
    return mesh.shape["hor"] == 8 and mesh.shape["dep"] == 2


def chosen(mesh, residual, focus_bins, layer_class):
    shape = residual.shape
    if fits_kernel(mesh) and shape[1] % 8 == 0 and shape[2] == 1024 and shape[0] % GROUP == 0:
        return kernel_body(residual, focus_bins, layer_class)
    return body(residual, focus_bins, layer_class)


def solution(mesh):
    return jax.shard_map(
        functools.partial(chosen, mesh),
        mesh=mesh,
        in_specs=(P(("grp", "dep"), "hor", None), P(("grp", "dep"), "hor", None), P("grp")),
        out_specs=P(("grp", "dep"), "hor", None),
        check_vma=False,
    )
```

```python
import functools
import math

import jax
import jax.numpy as jnp
import ml_dtypes
import numpy as np
from jax import lax
from jax.experimental import pallas as pl
from jax.experimental.pallas import tpu as pltpu
from jax.sharding import PartitionSpec as P

damping = 0.01
smoothing = 1.0
coupling_scale = 1.0
weight_base = 0.5
weight_step = 0.2
focus_base = 0.5
focus_step = 0.09242
highest = lax.Precision.HIGHEST


def partner_2(value, axis, distance):
    mask = 2**distance
    pairs = [(source, source ^ mask) for source in range(lax.axis_size(axis))]
    return lax.ppermute(value, axis, pairs)


def depth_weights(layer_class):
    return weight_base * jnp.exp(weight_step * layer_class.astype(jnp.float32))


def focusing(focus_bins):
    return focus_base * jnp.exp(focus_step * focus_bins.astype(jnp.float32))


def couplings(weights):
    inner = coupling_scale * weights[:-1] * weights[1:]
    zero_end = jnp.zeros((1,), jnp.float32)
    return (jnp.concatenate([zero_end, inner]), jnp.concatenate([inner, zero_end]))


def symbol(frequency, length):
    return 2.0 - 2.0 * jnp.cos(frequency * (2.0 * math.pi / length))


def cas_table(length):
    position = jnp.arange(length, dtype=jnp.int32)
    product = position[:, None] * position[None, :] % length
    angles = product.astype(jnp.float32) * (2.0 * math.pi / length)
    return jnp.cos(angles) + jnp.sin(angles)


def shift_down(values, distance, fill_value):
    filler = jnp.full(values.shape[:-2] + (distance, values.shape[-1]), fill_value, values.dtype)
    return jnp.concatenate([filler, values[..., :-distance, :]], axis=-2)


def shift_up(values, distance, fill_value):
    filler = jnp.full(values.shape[:-2] + (distance, values.shape[-1]), fill_value, values.dtype)
    return jnp.concatenate([values[..., distance:, :], filler], axis=-2)


def reduce_step(lower, middle, upper, source, rows_below, rows_above):
    lower_below, middle_below, upper_below, source_below = rows_below
    lower_above, middle_above, upper_above, source_above = rows_above
    ratio_below = -lower / middle_below
    ratio_above = -upper / middle_above
    new_lower = ratio_below * lower_below
    new_middle = middle + ratio_below * upper_below + ratio_above * lower_above
    new_upper = ratio_above * upper_above
    new_source = source + ratio_below * source_below + ratio_above * source_above
    return (new_lower, new_middle, new_upper, new_source)


def local_solve(lower, middle, upper, source):
    layer_count = middle.shape[0]
    distance = 1
    while distance < layer_count:
        rows_below = (
            shift_down(lower, distance, 0.0),
            shift_down(middle, distance, 1.0),
            shift_down(upper, distance, 0.0),
            shift_down(source, distance, 0.0),
        )
        rows_above = (
            shift_up(lower, distance, 0.0),
            shift_up(middle, distance, 1.0),
            shift_up(upper, distance, 0.0),
            shift_up(source, distance, 0.0),
        )
        lower, middle, upper, source = reduce_step(
            lower, middle, upper, source, rows_below, rows_above
        )
        distance = distance * 2
    return source / middle


def body(residual, focus_bins, layer_class):
    depth_rows, y_rows, x_cells = residual.shape
    hor_count = lax.axis_size("hor")
    y_cells = y_rows * hor_count
    focus_map = focusing(focus_bins)
    scaled = focus_map * residual
    weights = depth_weights(layer_class)
    couple_prev, couple_next = couplings(weights)
    first_row = lax.axis_index("dep") * depth_rows
    table_x = cas_table(x_cells)
    table_y = cas_table(y_cells)
    symbol_y = symbol(jnp.arange(y_cells, dtype=jnp.float32), y_cells)
    block_width = x_cells // hor_count
    block_index = lax.axis_index("hor")
    spectra = jnp.einsum(
        "zcx,xbj->bzcj", scaled, table_x.reshape(x_cells, hor_count, block_width), precision=highest
    )
    spectra = spectra.reshape(hor_count, depth_rows, y_rows * block_width)
    table_rows = table_y.reshape(hor_count, y_rows, y_cells)
    portion = lax.all_to_all(spectra, "hor", split_axis=0, concat_axis=0, tiled=True)
    item_count = portion.shape[1]
    arranged = portion.reshape(hor_count, item_count, y_rows, block_width)
    spectrum = jnp.einsum("hzcj,hcy->zjy", arranged, table_rows, precision=highest)
    spectrum = spectrum.reshape(depth_rows, block_width * y_cells)
    wave_x = (block_index * block_width + jnp.arange(block_width, dtype=jnp.int32)).astype(
        jnp.float32
    )
    wave_term = (
        damping + smoothing * (symbol_y[None, :] + symbol(wave_x, x_cells)[:, None])
    ).reshape(-1)
    weight_local = lax.dynamic_slice_in_dim(weights, first_row, depth_rows)
    prev_local = lax.dynamic_slice_in_dim(couple_prev, first_row, depth_rows)
    next_local = lax.dynamic_slice_in_dim(couple_next, first_row, depth_rows)
    middle = weight_local[:, None] * wave_term[None, :] + (prev_local + next_local)[:, None]
    lower = jnp.broadcast_to(-prev_local[:, None], middle.shape)
    upper = jnp.broadcast_to(-next_local[:, None], middle.shape)
    row_index = jnp.arange(depth_rows, dtype=jnp.int32)
    edge_term = jnp.where(row_index == 0, prev_local[0], 0.0) + jnp.where(
        row_index == depth_rows - 1, next_local[depth_rows - 1], 0.0
    )
    source = jnp.stack([spectrum, jnp.broadcast_to(edge_term[:, None], spectrum.shape)])
    solutions = local_solve(lower, middle, upper, source)
    base_part = solutions[0]
    response = solutions[1]
    edge_row = (1 - lax.axis_index("dep")) * (depth_rows - 1)
    base_edge = lax.dynamic_index_in_dim(base_part, edge_row, 0, keepdims=False)
    response_edge = lax.dynamic_index_in_dim(response, edge_row, 0, keepdims=False)
    partner = partner_2(jnp.stack([base_edge, response_edge]), "dep", 0)
    divisor = 1.0 - response_edge * partner[1]
    interface = (partner[0] + partner[1] * base_edge) / divisor
    solved = base_part + response * interface[None, :]
    solved = solved.reshape(depth_rows, block_width, y_cells)
    returned = jnp.einsum(
        "zjk,khc->hzcj", solved, table_y.reshape(y_cells, hor_count, y_rows), precision=highest
    )
    returned = returned.reshape(hor_count, depth_rows, y_rows * block_width)
    table_back = table_x.reshape(hor_count, block_width, x_cells)
    portion = lax.all_to_all(returned, "hor", split_axis=0, concat_axis=0, tiled=True)
    item_count = portion.shape[1]
    arranged = portion.reshape(hor_count, item_count, y_rows, block_width)
    result_field = jnp.einsum("bzcj,bjx->zcx", arranged, table_back, precision=highest)
    return focus_map * result_field / (x_cells * y_cells)

MESH = pl.DeviceIdType.MESH


def split_table(length):
    position = np.arange(length)
    angles = (position[:, None] * position[None, :] % length) * (2.0 * math.pi / length)
    table = np.cos(angles) + np.sin(angles)
    high = table.astype(ml_dtypes.bfloat16)
    low = (table - high.astype(np.float64)).astype(ml_dtypes.bfloat16)
    return high, low


def split_values(values):
    high = values.astype(jnp.bfloat16)
    low = (values - high.astype(jnp.float32)).astype(jnp.bfloat16)
    return high, low


def dot32(left, right):
    return jnp.dot(left, right, preferred_element_type=jnp.float32)


def kernel(
    residual,
    bins,
    classes,
    table_high,
    table_low,
    back_high,
    back_low,
    table_y,
    wave_x,
    wave_y,
    result,
    res_v,
    bins_v,
    classes_v,
    table_y_v,
    wave_x_v,
    wave_y_v,
    high_v,
    low_v,
    back_high_v,
    back_low_v,
    focus_v,
    field_v,
    send_a,
    recv_a,
    send_b,
    recv_b,
    weights,
    inverse,
    factor,
    packed_inverse,
    packed_factor,
    spectrum,
    upper_part,
    gain_here,
    gain_there,
    edge_out,
    edge_in,
    load_sem,
    table_sem,
    send_a_sem,
    recv_a_sem,
    send_b_sem,
    recv_b_sem,
    edge_send_sem,
    edge_recv_sem,
    out_sem,
):
    _, count, pairs, y_rows, width = send_a.shape
    layers = 2 * pairs
    y_cells = count * y_rows
    plane = (y_cells // 8, 8, width)
    rows = layers * y_rows
    me = lax.axis_index("hor")
    half = lax.axis_index("dep")
    near = me // 4
    far = 1 - near

    barrier = pltpu.get_barrier_semaphore()
    for step in range(1, count):
        pl.semaphore_signal(
            barrier, inc=1, device_id={"hor": lax.rem(me + step, count)}, device_id_type=MESH
        )
    pl.semaphore_signal(barrier, inc=1, device_id={"dep": 1 - half}, device_id_type=MESH)

    def table_copy(kind, block):
        source = (table_high, table_low, back_high, back_low)[kind]
        target = (high_v, low_v, back_high_v, back_low_v)[kind]
        return pltpu.make_async_copy(
            source.at[block], target.at[block], table_sem.at[kind, block]
        )

    loads = [
        pltpu.make_async_copy(residual, res_v, load_sem.at[0]),
        pltpu.make_async_copy(bins, bins_v, load_sem.at[1]),
    ]
    late_loads = [
        pltpu.make_async_copy(classes, classes_v, load_sem.at[2]),
        pltpu.make_async_copy(table_y, table_y_v, load_sem.at[3]),
        pltpu.make_async_copy(wave_x.at[me], wave_x_v, load_sem.at[4]),
        pltpu.make_async_copy(wave_y, wave_y_v, load_sem.at[5]),
    ]
    blocks = [far, near, 2 + far, 2 + near]
    for load in loads:
        load.start()
    for block in blocks:
        table_copy(0, block).start()
        table_copy(1, block).start()
    for load in late_loads:
        load.start()

    lane = lax.broadcasted_iota(jnp.int32, (y_cells, width), 1)
    low_lanes = lane < width // 2

    def turn(value):
        return pltpu.roll(value, width // 2, 1)

    def mix(first, second):
        return (
            jnp.where(low_lanes, first, turn(second)),
            jnp.where(low_lanes, turn(first), second),
        )

    for load in loads:
        load.wait()
    focus_map = focus_base * jnp.exp(focus_step * bins_v[...].astype(jnp.float32))
    scaled = (focus_map * res_v[...]).reshape(rows, count * width)
    focus_v[...] = focus_map * (1.0 / (count * width * y_cells))
    high, low = split_values(scaled)
    stacked = jnp.concatenate([high, low], axis=0)

    def send_forward(chunk, target):
        return pltpu.make_async_remote_copy(
            src_ref=send_a.at[chunk, target],
            dst_ref=recv_a.at[chunk, me],
            send_sem=send_a_sem.at[chunk, target],
            recv_sem=recv_a_sem.at[chunk, me],
            device_id={"hor": target},
            device_id_type=MESH,
        )

    def wait_forward(chunk, source):
        pltpu.make_async_remote_copy(
            src_ref=send_a.at[chunk, source],
            dst_ref=recv_a.at[chunk, source],
            send_sem=send_a_sem.at[chunk, source],
            recv_sem=recv_a_sem.at[chunk, source],
            device_id={"hor": source},
            device_id_type=MESH,
        ).wait_recv()

    def send_back(chunk, target):
        return pltpu.make_async_remote_copy(
            src_ref=send_b.at[chunk, target],
            dst_ref=recv_b.at[chunk, me],
            send_sem=send_b_sem.at[chunk, target],
            recv_sem=recv_b_sem.at[chunk, me],
            device_id={"hor": target},
            device_id_type=MESH,
        )

    def wait_back(chunk, source):
        pltpu.make_async_remote_copy(
            src_ref=send_b.at[chunk, source],
            dst_ref=recv_b.at[chunk, source],
            send_sem=send_b_sem.at[chunk, source],
            recv_sem=recv_b_sem.at[chunk, source],
            device_id={"hor": source},
            device_id_type=MESH,
        ).wait_recv()

    far_targets = [4 * far + lax.rem(me + step, 4) for step in range(4)]
    near_targets = [4 * near + lax.rem(me + step, 4) for step in range(1, 4)]
    others = far_targets + near_targets

    for step, block in enumerate(blocks):
        chunk = step // 2
        side = far if step % 2 == 0 else near
        table_copy(0, block).wait()
        table_copy(1, block).wait()
        first = dot32(stacked, high_v[block])
        value = first[:rows] + first[rows:] + dot32(high, low_v[block])
        for pair in range(2):
            part = value[:, pair * width : (pair + 1) * width]
            even, odd = mix(part[: rows // 2], part[rows // 2 :])
            send_a[chunk, 4 * side + 2 * pair] = even.reshape(pairs, y_rows, width)
            send_a[chunk, 4 * side + 2 * pair + 1] = odd.reshape(pairs, y_rows, width)
        if step == 0:
            pl.semaphore_wait(barrier, count)
        for target in far_targets if step % 2 == 0 else near_targets:
            send_forward(chunk, target).start()
        if step % 2 == 1:
            recv_a[chunk, me] = send_a[chunk, me]

    for kind in (2, 3):
        for block in range(4):
            table_copy(kind, block).start()

    for load in late_loads:
        load.wait()
    for layer in range(2 * layers):
        index = jnp.full((8, width), classes_v[0, layer], jnp.int32).astype(jnp.float32)
        weights[layer] = weight_base * jnp.exp(weight_step * index)

    def layer_of(place):
        return place + half * (layers - 1 - 2 * place)

    def coupling_after(place):
        here = half * layers + layer_of(place)
        return coupling_scale * weights[here] * weights[here + 1 - 2 * half]

    wave = damping + smoothing * (wave_y_v[...] + wave_x_v[...][None])

    def pivot_step(place, carried):
        here = weights[half * layers + layer_of(place)]
        excess = here[None] * wave + carried
        after = coupling_after(place)[None]
        reciprocal = 1.0 / (excess + after)
        inverse[layer_of(place)] = reciprocal
        scaled_after = after * reciprocal
        factor[layer_of(place)] = scaled_after
        edge_out[0] = excess
        return scaled_after * excess

    lax.fori_loop(0, layers, pivot_step, jnp.zeros(plane, jnp.float32))

    def edge_copy(slot):
        return pltpu.make_async_remote_copy(
            src_ref=edge_out.at[slot],
            dst_ref=edge_in.at[slot],
            send_sem=edge_send_sem.at[slot],
            recv_sem=edge_recv_sem.at[slot],
            device_id={"dep": 1 - half},
            device_id_type=MESH,
        )

    edge_copy(0).start()

    def flat(value):
        return value.reshape(y_cells, width)

    def pack_step(row, carried):
        parts = mix(flat(inverse[row]), flat(inverse[row + pairs]))
        packed_inverse[0, row], packed_inverse[1, row] = (part.reshape(plane) for part in parts)
        parts = mix(flat(factor[row]), flat(factor[row + pairs]))
        packed_factor[0, row], packed_factor[1, row] = (part.reshape(plane) for part in parts)
        return carried

    lax.fori_loop(0, pairs, pack_step, 0)

    edge_copy(0).wait()
    after = coupling_after(layers - 1)[None]
    here = edge_out[0]
    there = edge_in[0]
    scale = 1.0 / (here * there + after * (here + there))
    for target, value in ((gain_here, (there + after) * scale), (gain_there, after * scale)):
        parts = mix(flat(value), flat(value))
        target[0], target[1] = (part.reshape(plane) for part in parts)

    low_plane = low_lanes.reshape(plane)
    first_lanes = jnp.logical_xor(low_plane, jnp.full(plane, half, jnp.int32) == 1)

    def turn_plane(value):
        return turn(flat(value)).reshape(plane)

    def row_of(place):
        return place + half * (pairs - 1 - 2 * place)

    def transform_y(first, second):
        upper, lower = split_values(jnp.concatenate([first, second], axis=1))
        return dot32(table_y_v[...], jnp.concatenate([upper, upper, lower], axis=0))

    for chunk in range(2):
        for source in others:
            wait_forward(chunk, source)
        for row in range(0, pairs, 2):
            value = transform_y(flat(recv_a[chunk, :, row]), flat(recv_a[chunk, :, row + 1]))
            spectrum[row] = value[:, :width].reshape(plane)
            spectrum[row + 1] = value[:, width:].reshape(plane)
        carried = jnp.zeros(plane, jnp.float32)
        for side in range(2):
            for place in range(pairs):
                row = row_of(place)
                value = spectrum[row] + carried
                spectrum[row] = value
                forwarded = packed_factor[chunk, row] * value
                carried = jnp.where(first_lanes, forwarded, 0.0)
                if side == 1:
                    carried = forwarded - carried
            carried = turn_plane(carried)
        edge_out[1 + chunk] = value
        edge_copy(1 + chunk).start()
        edge_copy(1 + chunk).wait()
        following = gain_here[chunk] * value + gain_there[chunk] * turn_plane(edge_in[1 + chunk])
        upper_part[row_of(pairs - 1)] = following
        for place in reversed(range(pairs - 1)):
            row = row_of(place)
            following = (
                packed_inverse[chunk, row] * spectrum[row] + packed_factor[chunk, row] * following
            )
            upper_part[row] = following
        following = turn_plane(following)
        for place in reversed(range(pairs)):
            row = row_of(place)
            following = (
                packed_inverse[chunk, row] * spectrum[row] + packed_factor[chunk, row] * following
            )
            spectrum[row] = jnp.where(first_lanes, following, upper_part[row])
        for row in range(0, pairs, 2):
            value = transform_y(flat(spectrum[row]), flat(spectrum[row + 1]))
            send_b[chunk, :, row] = value[:, :width].reshape(count, y_rows, width)
            send_b[chunk, :, row + 1] = value[:, width:].reshape(count, y_rows, width)
        for target in others:
            send_back(chunk, target).start()
        recv_b[chunk, me] = send_b[chunk, me]

    for kind in (2, 3):
        for block in range(4):
            table_copy(kind, block).wait()

    def gathered(chunk, side):
        tops = []
        bottoms = []
        for pair in range(2):
            even = flat(recv_b[chunk, 4 * side + 2 * pair])
            odd = flat(recv_b[chunk, 4 * side + 2 * pair + 1])
            top, bottom = mix(even, odd)
            tops.append(top)
            bottoms.append(bottom)
        value = jnp.concatenate(
            [jnp.concatenate(tops, axis=1), jnp.concatenate(bottoms, axis=1)], axis=0
        )
        upper, lower = split_values(value)
        return jnp.concatenate([upper, lower], axis=0), upper

    def product(stacked, upper, block, columns):
        first = dot32(stacked, back_high_v[block, :, columns])
        return first[:rows] + first[rows:] + dot32(upper, back_low_v[block, :, columns])

    def out_copy(index):
        columns = pl.ds(index * 2 * width, 2 * width)
        return pltpu.make_async_copy(
            field_v.at[:, :, columns], result.at[:, :, columns], out_sem.at[index]
        )

    for step in range(4):
        chunk = step // 2
        side = near if step % 2 == 0 else far
        for source in near_targets if step % 2 == 0 else far_targets:
            wait_back(chunk, source)
        pieces = gathered(chunk, side)
        for index in range(count // 2):
            columns = slice(index * 2 * width, (index + 1) * 2 * width)
            total = product(*pieces, 2 * chunk + side, columns).reshape(layers, y_rows, 2 * width)
            if step > 0:
                total = total + field_v[:, :, columns]
            if step == 3:
                total = total * focus_v[:, :, columns]
            field_v[:, :, columns] = total
            if step == 3:
                out_copy(index).start()

    for chunk in range(2):
        for target in others:
            send_forward(chunk, target).wait_send()
            send_back(chunk, target).wait_send()
    for index in range(count // 2):
        out_copy(index).wait()


def kernel_body(residual, focus_bins, layer_class):
    layers, y_rows, x_cells = residual.shape
    count = lax.axis_size("hor")
    width = x_cells // count
    y_cells = y_rows * count
    forward = []
    backward = []
    for table in split_table(x_cells):
        table = table.reshape(x_cells, count, 2, width // 2).transpose(2, 1, 3, 0)
        table = np.ascontiguousarray(table.reshape(4, 2 * width, x_cells))
        backward.append(table)
        forward.append(np.ascontiguousarray(table.transpose(0, 2, 1)))
    high_y, low_y = split_table(y_cells)
    table_y = np.concatenate([high_y, low_y, high_y], axis=1)
    wave_x = 2.0 - 2.0 * np.cos(np.arange(x_cells) * (2.0 * math.pi / x_cells))
    wave_x = np.broadcast_to(wave_x.reshape(count, 1, width), (count, 8, width)).astype(np.float32)
    wave_y = 2.0 - 2.0 * np.cos(np.arange(y_cells) * (2.0 * math.pi / y_cells))
    wave_y = np.broadcast_to(wave_y[:, None], (y_cells, width)).astype(np.float32)
    wave_y = wave_y.reshape(y_cells // 8, 8, width)
    pairs = layers // 2
    block = (2, count, pairs, y_rows, width)
    plane = (y_cells // 8, 8, width)
    f32, bf16, dma = jnp.float32, jnp.bfloat16, pltpu.SemaphoreType.DMA
    return pl.pallas_call(
        kernel,
        out_shape=jax.ShapeDtypeStruct(residual.shape, f32),
        in_specs=[pl.BlockSpec(memory_space=pl.ANY)] * 10,
        out_specs=pl.BlockSpec(memory_space=pl.ANY),
        scratch_shapes=[
            pltpu.VMEM(residual.shape, f32),
            pltpu.VMEM(residual.shape, jnp.int32),
            pltpu.SMEM((1, 2 * layers), jnp.int32),
            pltpu.VMEM(table_y.shape, bf16),
            pltpu.VMEM((8, width), f32),
            pltpu.VMEM(plane, f32),
            pltpu.VMEM(forward[0].shape, bf16),
            pltpu.VMEM(forward[1].shape, bf16),
            pltpu.VMEM(backward[0].shape, bf16),
            pltpu.VMEM(backward[1].shape, bf16),
            pltpu.VMEM(residual.shape, f32),
            pltpu.VMEM(residual.shape, f32),
            pltpu.VMEM(block, f32),
            pltpu.VMEM(block, f32),
            pltpu.VMEM(block, f32),
            pltpu.VMEM(block, f32),
            pltpu.VMEM((2 * layers, 8, width), f32),
            pltpu.VMEM((layers,) + plane, f32),
            pltpu.VMEM((layers,) + plane, f32),
            pltpu.VMEM((2, pairs) + plane, f32),
            pltpu.VMEM((2, pairs) + plane, f32),
            pltpu.VMEM((pairs,) + plane, f32),
            pltpu.VMEM((pairs,) + plane, f32),
            pltpu.VMEM((2,) + plane, f32),
            pltpu.VMEM((2,) + plane, f32),
            pltpu.VMEM((3,) + plane, f32),
            pltpu.VMEM((3,) + plane, f32),
            dma((6,)),
            dma((4, 4)),
            dma((2, count)),
            dma((2, count)),
            dma((2, count)),
            dma((2, count)),
            dma((3,)),
            dma((3,)),
            dma((count // 2,)),
        ],
        compiler_params=pltpu.CompilerParams(
            collective_id=0, has_side_effects=True, vmem_limit_bytes=64 * 2**20
        ),
        cost_estimate=pl.CostEstimate(
            flops=2 * 6 * layers * y_rows * x_cells * x_cells,
            bytes_accessed=10 * 2**20,
            transcendentals=layers * y_rows * x_cells,
        ),
    )(
        residual,
        focus_bins,
        layer_class.reshape(1, -1),
        jnp.asarray(forward[0]),
        jnp.asarray(forward[1]),
        jnp.asarray(backward[0]),
        jnp.asarray(backward[1]),
        jnp.asarray(table_y),
        jnp.asarray(wave_x),
        jnp.asarray(wave_y),
    )


def fits_kernel(mesh):
    return mesh.shape["hor"] == 8 and mesh.shape["dep"] == 2


def chosen(mesh, residual, focus_bins, layer_class):
    shape = residual.shape
    if fits_kernel(mesh) and shape == (16, 8, 1024):
        return kernel_body(residual, focus_bins, layer_class)
    return body(residual, focus_bins, layer_class)


def solution(mesh):
    return jax.shard_map(
        functools.partial(chosen, mesh),
        mesh=mesh,
        in_specs=(P(("grp", "dep"), "hor", None), P(("grp", "dep"), "hor", None), P("grp")),
        out_specs=P(("grp", "dep"), "hor", None),
        check_vma=False,
    )
```

```python
import functools
import math

import jax
import jax.numpy as jnp
import ml_dtypes
import numpy as np
from jax import lax
from jax.experimental import pallas as pl
from jax.experimental.pallas import tpu as pltpu
from jax.sharding import PartitionSpec as P

damping = 0.01
smoothing = 1.0
coupling_scale = 1.0
weight_base = 0.5
weight_step = 0.2
focus_base = 0.5
focus_step = 0.09242
highest = lax.Precision.HIGHEST


def partner_2(value, axis, distance):
    mask = 2**distance
    pairs = [(source, source ^ mask) for source in range(lax.axis_size(axis))]
    return lax.ppermute(value, axis, pairs)


def depth_weights(layer_class):
    return weight_base * jnp.exp(weight_step * layer_class.astype(jnp.float32))


def focusing(focus_bins):
    return focus_base * jnp.exp(focus_step * focus_bins.astype(jnp.float32))


def couplings(weights):
    inner = coupling_scale * weights[:-1] * weights[1:]
    zero_end = jnp.zeros((1,), jnp.float32)
    return (jnp.concatenate([zero_end, inner]), jnp.concatenate([inner, zero_end]))


def symbol(frequency, length):
    return 2.0 - 2.0 * jnp.cos(frequency * (2.0 * math.pi / length))


def cas_table(length):
    position = jnp.arange(length, dtype=jnp.int32)
    product = position[:, None] * position[None, :] % length
    angles = product.astype(jnp.float32) * (2.0 * math.pi / length)
    return jnp.cos(angles) + jnp.sin(angles)


def shift_down(values, distance, fill_value):
    filler = jnp.full(values.shape[:-2] + (distance, values.shape[-1]), fill_value, values.dtype)
    return jnp.concatenate([filler, values[..., :-distance, :]], axis=-2)


def shift_up(values, distance, fill_value):
    filler = jnp.full(values.shape[:-2] + (distance, values.shape[-1]), fill_value, values.dtype)
    return jnp.concatenate([values[..., distance:, :], filler], axis=-2)


def reduce_step(lower, middle, upper, source, rows_below, rows_above):
    lower_below, middle_below, upper_below, source_below = rows_below
    lower_above, middle_above, upper_above, source_above = rows_above
    ratio_below = -lower / middle_below
    ratio_above = -upper / middle_above
    new_lower = ratio_below * lower_below
    new_middle = middle + ratio_below * upper_below + ratio_above * lower_above
    new_upper = ratio_above * upper_above
    new_source = source + ratio_below * source_below + ratio_above * source_above
    return (new_lower, new_middle, new_upper, new_source)


def local_solve(lower, middle, upper, source):
    layer_count = middle.shape[0]
    distance = 1
    while distance < layer_count:
        rows_below = (
            shift_down(lower, distance, 0.0),
            shift_down(middle, distance, 1.0),
            shift_down(upper, distance, 0.0),
            shift_down(source, distance, 0.0),
        )
        rows_above = (
            shift_up(lower, distance, 0.0),
            shift_up(middle, distance, 1.0),
            shift_up(upper, distance, 0.0),
            shift_up(source, distance, 0.0),
        )
        lower, middle, upper, source = reduce_step(
            lower, middle, upper, source, rows_below, rows_above
        )
        distance = distance * 2
    return source / middle


def body(residual, focus_bins, layer_class):
    depth_rows, y_rows, x_cells = residual.shape
    hor_count = lax.axis_size("hor")
    y_cells = y_rows * hor_count
    focus_map = focusing(focus_bins)
    scaled = focus_map * residual
    weights = depth_weights(layer_class)
    couple_prev, couple_next = couplings(weights)
    first_row = lax.axis_index("dep") * depth_rows
    table_x = cas_table(x_cells)
    table_y = cas_table(y_cells)
    symbol_y = symbol(jnp.arange(y_cells, dtype=jnp.float32), y_cells)
    block_width = x_cells // hor_count
    block_index = lax.axis_index("hor")
    spectra = jnp.einsum(
        "zcx,xbj->bzcj", scaled, table_x.reshape(x_cells, hor_count, block_width), precision=highest
    )
    spectra = spectra.reshape(hor_count, depth_rows, y_rows * block_width)
    table_rows = table_y.reshape(hor_count, y_rows, y_cells)
    portion = lax.all_to_all(spectra, "hor", split_axis=0, concat_axis=0, tiled=True)
    item_count = portion.shape[1]
    arranged = portion.reshape(hor_count, item_count, y_rows, block_width)
    spectrum = jnp.einsum("hzcj,hcy->zjy", arranged, table_rows, precision=highest)
    spectrum = spectrum.reshape(depth_rows, block_width * y_cells)
    wave_x = (block_index * block_width + jnp.arange(block_width, dtype=jnp.int32)).astype(
        jnp.float32
    )
    wave_term = (
        damping + smoothing * (symbol_y[None, :] + symbol(wave_x, x_cells)[:, None])
    ).reshape(-1)
    weight_local = lax.dynamic_slice_in_dim(weights, first_row, depth_rows)
    prev_local = lax.dynamic_slice_in_dim(couple_prev, first_row, depth_rows)
    next_local = lax.dynamic_slice_in_dim(couple_next, first_row, depth_rows)
    middle = weight_local[:, None] * wave_term[None, :] + (prev_local + next_local)[:, None]
    lower = jnp.broadcast_to(-prev_local[:, None], middle.shape)
    upper = jnp.broadcast_to(-next_local[:, None], middle.shape)
    row_index = jnp.arange(depth_rows, dtype=jnp.int32)
    edge_term = jnp.where(row_index == 0, prev_local[0], 0.0) + jnp.where(
        row_index == depth_rows - 1, next_local[depth_rows - 1], 0.0
    )
    source = jnp.stack([spectrum, jnp.broadcast_to(edge_term[:, None], spectrum.shape)])
    solutions = local_solve(lower, middle, upper, source)
    base_part = solutions[0]
    response = solutions[1]
    edge_row = (1 - lax.axis_index("dep")) * (depth_rows - 1)
    base_edge = lax.dynamic_index_in_dim(base_part, edge_row, 0, keepdims=False)
    response_edge = lax.dynamic_index_in_dim(response, edge_row, 0, keepdims=False)
    partner = partner_2(jnp.stack([base_edge, response_edge]), "dep", 0)
    divisor = 1.0 - response_edge * partner[1]
    interface = (partner[0] + partner[1] * base_edge) / divisor
    solved = base_part + response * interface[None, :]
    solved = solved.reshape(depth_rows, block_width, y_cells)
    returned = jnp.einsum(
        "zjk,khc->hzcj", solved, table_y.reshape(y_cells, hor_count, y_rows), precision=highest
    )
    returned = returned.reshape(hor_count, depth_rows, y_rows * block_width)
    table_back = table_x.reshape(hor_count, block_width, x_cells)
    portion = lax.all_to_all(returned, "hor", split_axis=0, concat_axis=0, tiled=True)
    item_count = portion.shape[1]
    arranged = portion.reshape(hor_count, item_count, y_rows, block_width)
    result_field = jnp.einsum("bzcj,bjx->zcx", arranged, table_back, precision=highest)
    return focus_map * result_field / (x_cells * y_cells)

MESH = pl.DeviceIdType.MESH


def split_table(length):
    position = np.arange(length)
    angles = (position[:, None] * position[None, :] % length) * (2.0 * math.pi / length)
    table = np.cos(angles) + np.sin(angles)
    high = table.astype(ml_dtypes.bfloat16)
    low = (table - high.astype(np.float64)).astype(ml_dtypes.bfloat16)
    return high, low


def split_values(values):
    high = values.astype(jnp.bfloat16)
    low = (values - high.astype(jnp.float32)).astype(jnp.bfloat16)
    return high, low


def dot32(left, right):
    return jnp.dot(left, right, preferred_element_type=jnp.float32)


def kernel(
    residual,
    bins,
    classes,
    table_high,
    table_low,
    back_high,
    back_low,
    table_y,
    wave_x,
    wave_y,
    result,
    res_v,
    bins_v,
    classes_v,
    table_y_v,
    wave_x_v,
    wave_y_v,
    high_v,
    low_v,
    back_high_v,
    back_low_v,
    focus_v,
    field_v,
    send_a,
    recv_a,
    send_b,
    recv_b,
    weights,
    inverse,
    factor,
    packed_inverse,
    packed_factor,
    spectrum,
    upper_part,
    gain_here,
    gain_there,
    edge_out,
    edge_in,
    load_sem,
    table_sem,
    send_a_sem,
    recv_a_sem,
    send_b_sem,
    recv_b_sem,
    edge_send_sem,
    edge_recv_sem,
    out_sem,
):
    _, count, pairs, y_rows, width = send_a.shape
    layers = 2 * pairs
    y_cells = count * y_rows
    plane = (y_cells // 8, 8, width)
    rows = layers * y_rows
    me = lax.axis_index("hor")
    half = lax.axis_index("dep")
    near = me // 4
    far = 1 - near

    barrier = pltpu.get_barrier_semaphore()
    for step in range(1, count):
        pl.semaphore_signal(
            barrier, inc=1, device_id={"hor": lax.rem(me + step, count)}, device_id_type=MESH
        )
    pl.semaphore_signal(barrier, inc=1, device_id={"dep": 1 - half}, device_id_type=MESH)

    def table_copy(kind, block):
        source = (table_high, table_low, back_high, back_low)[kind]
        target = (high_v, low_v, back_high_v, back_low_v)[kind]
        return pltpu.make_async_copy(
            source.at[block], target.at[block], table_sem.at[kind, block]
        )

    loads = [
        pltpu.make_async_copy(residual, res_v, load_sem.at[0]),
        pltpu.make_async_copy(bins, bins_v, load_sem.at[1]),
    ]
    late_loads = [
        pltpu.make_async_copy(classes, classes_v, load_sem.at[2]),
        pltpu.make_async_copy(table_y, table_y_v, load_sem.at[3]),
        pltpu.make_async_copy(wave_x.at[me], wave_x_v, load_sem.at[4]),
        pltpu.make_async_copy(wave_y, wave_y_v, load_sem.at[5]),
    ]
    blocks = [far, near, 2 + far, 2 + near]
    for load in loads:
        load.start()
    for block in blocks:
        table_copy(0, block).start()
        table_copy(1, block).start()
    for load in late_loads:
        load.start()

    lane = lax.broadcasted_iota(jnp.int32, (y_cells, width), 1)
    low_lanes = lane < width // 2

    def turn(value):
        return pltpu.roll(value, width // 2, 1)

    def mix(first, second):
        return (
            jnp.where(low_lanes, first, turn(second)),
            jnp.where(low_lanes, turn(first), second),
        )

    for load in loads:
        load.wait()
    focus_map = focus_base * jnp.exp(focus_step * bins_v[...].astype(jnp.float32))
    scaled = (focus_map * res_v[...]).reshape(rows, count * width)
    focus_v[...] = focus_map * (1.0 / (count * width * y_cells))
    high, low = split_values(scaled)
    stacked = jnp.concatenate([high, low], axis=0)

    def send_forward(chunk, target):
        return pltpu.make_async_remote_copy(
            src_ref=send_a.at[chunk, target],
            dst_ref=recv_a.at[chunk, me],
            send_sem=send_a_sem.at[chunk, target],
            recv_sem=recv_a_sem.at[chunk, me],
            device_id={"hor": target},
            device_id_type=MESH,
        )

    def wait_forward(chunk, source):
        pltpu.make_async_remote_copy(
            src_ref=send_a.at[chunk, source],
            dst_ref=recv_a.at[chunk, source],
            send_sem=send_a_sem.at[chunk, source],
            recv_sem=recv_a_sem.at[chunk, source],
            device_id={"hor": source},
            device_id_type=MESH,
        ).wait_recv()

    def send_back(chunk, target):
        return pltpu.make_async_remote_copy(
            src_ref=send_b.at[chunk, target],
            dst_ref=recv_b.at[chunk, me],
            send_sem=send_b_sem.at[chunk, target],
            recv_sem=recv_b_sem.at[chunk, me],
            device_id={"hor": target},
            device_id_type=MESH,
        )

    def wait_back(chunk, source):
        pltpu.make_async_remote_copy(
            src_ref=send_b.at[chunk, source],
            dst_ref=recv_b.at[chunk, source],
            send_sem=send_b_sem.at[chunk, source],
            recv_sem=recv_b_sem.at[chunk, source],
            device_id={"hor": source},
            device_id_type=MESH,
        ).wait_recv()

    far_targets = [4 * far + lax.rem(me + step, 4) for step in range(4)]
    near_targets = [4 * near + lax.rem(me + step, 4) for step in range(1, 4)]
    others = far_targets + near_targets

    for step, block in enumerate(blocks):
        chunk = step // 2
        side = far if step % 2 == 0 else near
        table_copy(0, block).wait()
        table_copy(1, block).wait()
        first = dot32(stacked, high_v[block])
        value = first[:rows] + first[rows:] + dot32(high, low_v[block])
        for pair in range(2):
            part = value[:, pair * width : (pair + 1) * width]
            even, odd = mix(part[: rows // 2], part[rows // 2 :])
            send_a[chunk, 4 * side + 2 * pair] = even.reshape(pairs, y_rows, width)
            send_a[chunk, 4 * side + 2 * pair + 1] = odd.reshape(pairs, y_rows, width)
        if step == 0:
            pl.semaphore_wait(barrier, count)
        if chunk == 0:
            for target in far_targets if step == 0 else near_targets:
                send_forward(0, target).start()
        if step % 2 == 1:
            recv_a[chunk, me] = send_a[chunk, me]

    for kind in (2, 3):
        for block in range(4):
            table_copy(kind, block).start()

    for load in late_loads:
        load.wait()
    for layer in range(2 * layers):
        index = jnp.full((8, width), classes_v[0, layer], jnp.int32).astype(jnp.float32)
        weights[layer] = weight_base * jnp.exp(weight_step * index)

    def layer_of(place):
        return place + half * (layers - 1 - 2 * place)

    def coupling_after(place):
        here = half * layers + layer_of(place)
        return coupling_scale * weights[here] * weights[here + 1 - 2 * half]

    wave = damping + smoothing * (wave_y_v[...] + wave_x_v[...][None])

    def pivot_step(place, carried):
        here = weights[half * layers + layer_of(place)]
        excess = here[None] * wave + carried
        after = coupling_after(place)[None]
        reciprocal = 1.0 / (excess + after)
        inverse[layer_of(place)] = reciprocal
        scaled_after = after * reciprocal
        factor[layer_of(place)] = scaled_after
        edge_out[0] = excess
        return scaled_after * excess

    lax.fori_loop(0, layers, pivot_step, jnp.zeros(plane, jnp.float32))

    def edge_copy(slot):
        return pltpu.make_async_remote_copy(
            src_ref=edge_out.at[slot],
            dst_ref=edge_in.at[slot],
            send_sem=edge_send_sem.at[slot],
            recv_sem=edge_recv_sem.at[slot],
            device_id={"dep": 1 - half},
            device_id_type=MESH,
        )

    edge_copy(0).start()

    def flat(value):
        return value.reshape(y_cells, width)

    def pack_step(row, carried):
        parts = mix(flat(inverse[row]), flat(inverse[row + pairs]))
        packed_inverse[0, row], packed_inverse[1, row] = (part.reshape(plane) for part in parts)
        parts = mix(flat(factor[row]), flat(factor[row + pairs]))
        packed_factor[0, row], packed_factor[1, row] = (part.reshape(plane) for part in parts)
        return carried

    lax.fori_loop(0, pairs, pack_step, 0)

    edge_copy(0).wait()
    after = coupling_after(layers - 1)[None]
    here = edge_out[0]
    there = edge_in[0]
    scale = 1.0 / (here * there + after * (here + there))
    for target, value in ((gain_here, (there + after) * scale), (gain_there, after * scale)):
        parts = mix(flat(value), flat(value))
        target[0], target[1] = (part.reshape(plane) for part in parts)

    for target in others:
        send_forward(0, target).wait_send()
        send_forward(1, target).start()

    low_plane = low_lanes.reshape(plane)
    first_lanes = jnp.logical_xor(low_plane, jnp.full(plane, half, jnp.int32) == 1)

    def turn_plane(value):
        return turn(flat(value)).reshape(plane)

    def row_of(place):
        return place + half * (pairs - 1 - 2 * place)

    def transform_y(first, second):
        upper, lower = split_values(jnp.concatenate([first, second], axis=1))
        return dot32(table_y_v[...], jnp.concatenate([upper, upper, lower], axis=0))

    for chunk in range(2):
        for source in others:
            wait_forward(chunk, source)
        for row in range(0, pairs, 2):
            value = transform_y(flat(recv_a[chunk, :, row]), flat(recv_a[chunk, :, row + 1]))
            spectrum[row] = value[:, :width].reshape(plane)
            spectrum[row + 1] = value[:, width:].reshape(plane)
        carried = jnp.zeros(plane, jnp.float32)
        for side in range(2):
            for place in range(pairs):
                row = row_of(place)
                value = spectrum[row] + carried
                spectrum[row] = value
                forwarded = packed_factor[chunk, row] * value
                carried = jnp.where(first_lanes, forwarded, 0.0)
                if side == 1:
                    carried = forwarded - carried
            carried = turn_plane(carried)
        edge_out[1 + chunk] = value
        edge_copy(1 + chunk).start()
        edge_copy(1 + chunk).wait()
        following = gain_here[chunk] * value + gain_there[chunk] * turn_plane(edge_in[1 + chunk])
        upper_part[row_of(pairs - 1)] = following
        for place in reversed(range(pairs - 1)):
            row = row_of(place)
            following = (
                packed_inverse[chunk, row] * spectrum[row] + packed_factor[chunk, row] * following
            )
            upper_part[row] = following
        following = turn_plane(following)
        for place in reversed(range(pairs)):
            row = row_of(place)
            following = (
                packed_inverse[chunk, row] * spectrum[row] + packed_factor[chunk, row] * following
            )
            spectrum[row] = jnp.where(first_lanes, following, upper_part[row])
        for row in range(0, pairs, 2):
            value = transform_y(flat(spectrum[row]), flat(spectrum[row + 1]))
            send_b[chunk, :, row] = value[:, :width].reshape(count, y_rows, width)
            send_b[chunk, :, row + 1] = value[:, width:].reshape(count, y_rows, width)
        for target in others:
            send_back(chunk, target).start()
        recv_b[chunk, me] = send_b[chunk, me]

    for kind in (2, 3):
        for block in range(4):
            table_copy(kind, block).wait()

    def gathered(chunk, side):
        tops = []
        bottoms = []
        for pair in range(2):
            even = flat(recv_b[chunk, 4 * side + 2 * pair])
            odd = flat(recv_b[chunk, 4 * side + 2 * pair + 1])
            top, bottom = mix(even, odd)
            tops.append(top)
            bottoms.append(bottom)
        value = jnp.concatenate(
            [jnp.concatenate(tops, axis=1), jnp.concatenate(bottoms, axis=1)], axis=0
        )
        upper, lower = split_values(value)
        return jnp.concatenate([upper, lower], axis=0), upper

    def product(stacked, upper, block, columns):
        first = dot32(stacked, back_high_v[block, :, columns])
        return first[:rows] + first[rows:] + dot32(upper, back_low_v[block, :, columns])

    def out_copy(index):
        columns = pl.ds(index * 2 * width, 2 * width)
        return pltpu.make_async_copy(
            field_v.at[:, :, columns], result.at[:, :, columns], out_sem.at[index]
        )

    for step in range(4):
        chunk = step // 2
        side = near if step % 2 == 0 else far
        for source in near_targets if step % 2 == 0 else far_targets:
            wait_back(chunk, source)
        pieces = gathered(chunk, side)
        for index in range(count // 2):
            columns = slice(index * 2 * width, (index + 1) * 2 * width)
            total = product(*pieces, 2 * chunk + side, columns).reshape(layers, y_rows, 2 * width)
            if step > 0:
                total = total + field_v[:, :, columns]
            if step == 3:
                total = total * focus_v[:, :, columns]
            field_v[:, :, columns] = total
            if step == 3:
                out_copy(index).start()

    for chunk in range(2):
        for target in others:
            if chunk == 1:
                send_forward(1, target).wait_send()
            send_back(chunk, target).wait_send()
    for index in range(count // 2):
        out_copy(index).wait()


def kernel_body(residual, focus_bins, layer_class):
    layers, y_rows, x_cells = residual.shape
    count = lax.axis_size("hor")
    width = x_cells // count
    y_cells = y_rows * count
    forward = []
    backward = []
    for table in split_table(x_cells):
        table = table.reshape(x_cells, count, 2, width // 2).transpose(2, 1, 3, 0)
        table = np.ascontiguousarray(table.reshape(4, 2 * width, x_cells))
        backward.append(table)
        forward.append(np.ascontiguousarray(table.transpose(0, 2, 1)))
    high_y, low_y = split_table(y_cells)
    table_y = np.concatenate([high_y, low_y, high_y], axis=1)
    wave_x = 2.0 - 2.0 * np.cos(np.arange(x_cells) * (2.0 * math.pi / x_cells))
    wave_x = np.broadcast_to(wave_x.reshape(count, 1, width), (count, 8, width)).astype(np.float32)
    wave_y = 2.0 - 2.0 * np.cos(np.arange(y_cells) * (2.0 * math.pi / y_cells))
    wave_y = np.broadcast_to(wave_y[:, None], (y_cells, width)).astype(np.float32)
    wave_y = wave_y.reshape(y_cells // 8, 8, width)
    pairs = layers // 2
    block = (2, count, pairs, y_rows, width)
    plane = (y_cells // 8, 8, width)
    f32, bf16, dma = jnp.float32, jnp.bfloat16, pltpu.SemaphoreType.DMA
    return pl.pallas_call(
        kernel,
        out_shape=jax.ShapeDtypeStruct(residual.shape, f32),
        in_specs=[pl.BlockSpec(memory_space=pl.ANY)] * 10,
        out_specs=pl.BlockSpec(memory_space=pl.ANY),
        scratch_shapes=[
            pltpu.VMEM(residual.shape, f32),
            pltpu.VMEM(residual.shape, jnp.int32),
            pltpu.SMEM((1, 2 * layers), jnp.int32),
            pltpu.VMEM(table_y.shape, bf16),
            pltpu.VMEM((8, width), f32),
            pltpu.VMEM(plane, f32),
            pltpu.VMEM(forward[0].shape, bf16),
            pltpu.VMEM(forward[1].shape, bf16),
            pltpu.VMEM(backward[0].shape, bf16),
            pltpu.VMEM(backward[1].shape, bf16),
            pltpu.VMEM(residual.shape, f32),
            pltpu.VMEM(residual.shape, f32),
            pltpu.VMEM(block, f32),
            pltpu.VMEM(block, f32),
            pltpu.VMEM(block, f32),
            pltpu.VMEM(block, f32),
            pltpu.VMEM((2 * layers, 8, width), f32),
            pltpu.VMEM((layers,) + plane, f32),
            pltpu.VMEM((layers,) + plane, f32),
            pltpu.VMEM((2, pairs) + plane, f32),
            pltpu.VMEM((2, pairs) + plane, f32),
            pltpu.VMEM((pairs,) + plane, f32),
            pltpu.VMEM((pairs,) + plane, f32),
            pltpu.VMEM((2,) + plane, f32),
            pltpu.VMEM((2,) + plane, f32),
            pltpu.VMEM((3,) + plane, f32),
            pltpu.VMEM((3,) + plane, f32),
            dma((6,)),
            dma((4, 4)),
            dma((2, count)),
            dma((2, count)),
            dma((2, count)),
            dma((2, count)),
            dma((3,)),
            dma((3,)),
            dma((count // 2,)),
        ],
        compiler_params=pltpu.CompilerParams(
            collective_id=0, has_side_effects=True, vmem_limit_bytes=64 * 2**20
        ),
        cost_estimate=pl.CostEstimate(
            flops=2 * 6 * layers * y_rows * x_cells * x_cells,
            bytes_accessed=10 * 2**20,
            transcendentals=layers * y_rows * x_cells,
        ),
    )(
        residual,
        focus_bins,
        layer_class.reshape(1, -1),
        jnp.asarray(forward[0]),
        jnp.asarray(forward[1]),
        jnp.asarray(backward[0]),
        jnp.asarray(backward[1]),
        jnp.asarray(table_y),
        jnp.asarray(wave_x),
        jnp.asarray(wave_y),
    )


def fits_kernel(mesh):
    return mesh.shape["hor"] == 8 and mesh.shape["dep"] == 2


def chosen(mesh, residual, focus_bins, layer_class):
    shape = residual.shape
    if fits_kernel(mesh) and shape == (16, 8, 1024):
        return kernel_body(residual, focus_bins, layer_class)
    return body(residual, focus_bins, layer_class)


def solution(mesh):
    return jax.shard_map(
        functools.partial(chosen, mesh),
        mesh=mesh,
        in_specs=(P(("grp", "dep"), "hor", None), P(("grp", "dep"), "hor", None), P("grp")),
        out_specs=P(("grp", "dep"), "hor", None),
        check_vma=False,
    )
```

```python
import functools
import math

import jax
import jax.numpy as jnp
import ml_dtypes
import numpy as np
from jax import lax
from jax.experimental import pallas as pl
from jax.experimental.pallas import tpu as pltpu
from jax.sharding import PartitionSpec as P

damping = 0.01
smoothing = 1.0
coupling_scale = 1.0
weight_base = 0.5
weight_step = 0.2
focus_base = 0.5
focus_step = 0.09242
highest = lax.Precision.HIGHEST


def partner_2(value, axis, distance):
    mask = 2**distance
    pairs = [(source, source ^ mask) for source in range(lax.axis_size(axis))]
    return lax.ppermute(value, axis, pairs)


def depth_weights(layer_class):
    return weight_base * jnp.exp(weight_step * layer_class.astype(jnp.float32))


def focusing(focus_bins):
    return focus_base * jnp.exp(focus_step * focus_bins.astype(jnp.float32))


def couplings(weights):
    inner = coupling_scale * weights[:-1] * weights[1:]
    zero_end = jnp.zeros((1,), jnp.float32)
    return (jnp.concatenate([zero_end, inner]), jnp.concatenate([inner, zero_end]))


def symbol(frequency, length):
    return 2.0 - 2.0 * jnp.cos(frequency * (2.0 * math.pi / length))


def cas_table(length):
    position = jnp.arange(length, dtype=jnp.int32)
    product = position[:, None] * position[None, :] % length
    angles = product.astype(jnp.float32) * (2.0 * math.pi / length)
    return jnp.cos(angles) + jnp.sin(angles)


def shift_down(values, distance, fill_value):
    filler = jnp.full(values.shape[:-2] + (distance, values.shape[-1]), fill_value, values.dtype)
    return jnp.concatenate([filler, values[..., :-distance, :]], axis=-2)


def shift_up(values, distance, fill_value):
    filler = jnp.full(values.shape[:-2] + (distance, values.shape[-1]), fill_value, values.dtype)
    return jnp.concatenate([values[..., distance:, :], filler], axis=-2)


def reduce_step(lower, middle, upper, source, rows_below, rows_above):
    lower_below, middle_below, upper_below, source_below = rows_below
    lower_above, middle_above, upper_above, source_above = rows_above
    ratio_below = -lower / middle_below
    ratio_above = -upper / middle_above
    new_lower = ratio_below * lower_below
    new_middle = middle + ratio_below * upper_below + ratio_above * lower_above
    new_upper = ratio_above * upper_above
    new_source = source + ratio_below * source_below + ratio_above * source_above
    return (new_lower, new_middle, new_upper, new_source)


def local_solve(lower, middle, upper, source):
    layer_count = middle.shape[0]
    distance = 1
    while distance < layer_count:
        rows_below = (
            shift_down(lower, distance, 0.0),
            shift_down(middle, distance, 1.0),
            shift_down(upper, distance, 0.0),
            shift_down(source, distance, 0.0),
        )
        rows_above = (
            shift_up(lower, distance, 0.0),
            shift_up(middle, distance, 1.0),
            shift_up(upper, distance, 0.0),
            shift_up(source, distance, 0.0),
        )
        lower, middle, upper, source = reduce_step(
            lower, middle, upper, source, rows_below, rows_above
        )
        distance = distance * 2
    return source / middle


def body(residual, focus_bins, layer_class):
    depth_rows, y_rows, x_cells = residual.shape
    hor_count = lax.axis_size("hor")
    y_cells = y_rows * hor_count
    focus_map = focusing(focus_bins)
    scaled = focus_map * residual
    weights = depth_weights(layer_class)
    couple_prev, couple_next = couplings(weights)
    first_row = lax.axis_index("dep") * depth_rows
    table_x = cas_table(x_cells)
    table_y = cas_table(y_cells)
    symbol_y = symbol(jnp.arange(y_cells, dtype=jnp.float32), y_cells)
    block_width = x_cells // hor_count
    block_index = lax.axis_index("hor")
    spectra = jnp.einsum(
        "zcx,xbj->bzcj", scaled, table_x.reshape(x_cells, hor_count, block_width), precision=highest
    )
    spectra = spectra.reshape(hor_count, depth_rows, y_rows * block_width)
    table_rows = table_y.reshape(hor_count, y_rows, y_cells)
    portion = lax.all_to_all(spectra, "hor", split_axis=0, concat_axis=0, tiled=True)
    item_count = portion.shape[1]
    arranged = portion.reshape(hor_count, item_count, y_rows, block_width)
    spectrum = jnp.einsum("hzcj,hcy->zjy", arranged, table_rows, precision=highest)
    spectrum = spectrum.reshape(depth_rows, block_width * y_cells)
    wave_x = (block_index * block_width + jnp.arange(block_width, dtype=jnp.int32)).astype(
        jnp.float32
    )
    wave_term = (
        damping + smoothing * (symbol_y[None, :] + symbol(wave_x, x_cells)[:, None])
    ).reshape(-1)
    weight_local = lax.dynamic_slice_in_dim(weights, first_row, depth_rows)
    prev_local = lax.dynamic_slice_in_dim(couple_prev, first_row, depth_rows)
    next_local = lax.dynamic_slice_in_dim(couple_next, first_row, depth_rows)
    middle = weight_local[:, None] * wave_term[None, :] + (prev_local + next_local)[:, None]
    lower = jnp.broadcast_to(-prev_local[:, None], middle.shape)
    upper = jnp.broadcast_to(-next_local[:, None], middle.shape)
    row_index = jnp.arange(depth_rows, dtype=jnp.int32)
    edge_term = jnp.where(row_index == 0, prev_local[0], 0.0) + jnp.where(
        row_index == depth_rows - 1, next_local[depth_rows - 1], 0.0
    )
    source = jnp.stack([spectrum, jnp.broadcast_to(edge_term[:, None], spectrum.shape)])
    solutions = local_solve(lower, middle, upper, source)
    base_part = solutions[0]
    response = solutions[1]
    edge_row = (1 - lax.axis_index("dep")) * (depth_rows - 1)
    base_edge = lax.dynamic_index_in_dim(base_part, edge_row, 0, keepdims=False)
    response_edge = lax.dynamic_index_in_dim(response, edge_row, 0, keepdims=False)
    partner = partner_2(jnp.stack([base_edge, response_edge]), "dep", 0)
    divisor = 1.0 - response_edge * partner[1]
    interface = (partner[0] + partner[1] * base_edge) / divisor
    solved = base_part + response * interface[None, :]
    solved = solved.reshape(depth_rows, block_width, y_cells)
    returned = jnp.einsum(
        "zjk,khc->hzcj", solved, table_y.reshape(y_cells, hor_count, y_rows), precision=highest
    )
    returned = returned.reshape(hor_count, depth_rows, y_rows * block_width)
    table_back = table_x.reshape(hor_count, block_width, x_cells)
    portion = lax.all_to_all(returned, "hor", split_axis=0, concat_axis=0, tiled=True)
    item_count = portion.shape[1]
    arranged = portion.reshape(hor_count, item_count, y_rows, block_width)
    result_field = jnp.einsum("bzcj,bjx->zcx", arranged, table_back, precision=highest)
    return focus_map * result_field / (x_cells * y_cells)

MESH = pl.DeviceIdType.MESH


def split_table(length):
    position = np.arange(length)
    angles = (position[:, None] * position[None, :] % length) * (2.0 * math.pi / length)
    table = np.cos(angles) + np.sin(angles)
    high = table.astype(ml_dtypes.bfloat16)
    low = (table - high.astype(np.float64)).astype(ml_dtypes.bfloat16)
    return high, low


def split_values(values):
    high = values.astype(jnp.bfloat16)
    low = (values - high.astype(jnp.float32)).astype(jnp.bfloat16)
    return high, low


def dot32(left, right):
    return jnp.dot(left, right, preferred_element_type=jnp.float32)


def kernel(
    residual,
    bins,
    classes,
    table_high,
    table_low,
    back_high,
    back_low,
    result,
    res_v,
    bins_v,
    classes_v,
    table_y_v,
    high_v,
    low_v,
    back_high_v,
    back_low_v,
    focus_v,
    send_a,
    recv_a,
    send_b,
    recv_b,
    weights,
    inverse,
    factor,
    packed_inverse,
    packed_factor,
    response,
    packed_response,
    spectrum,
    upper_part,
    gain_here,
    gain_there,
    edge_out,
    edge_in,
    load_sem,
    table_sem,
    send_a_sem,
    recv_a_sem,
    send_b_sem,
    recv_b_sem,
    edge_send_sem,
    edge_recv_sem,
):
    _, count, pairs, y_rows, width = send_a.shape
    layers = 2 * pairs
    y_cells = count * y_rows
    plane = (y_cells // 8, 8, width)
    x_cells = count * width
    rows = layers * y_rows
    me = lax.axis_index("hor")
    half = lax.axis_index("dep")
    near = me // 4
    far = 1 - near

    barrier = pltpu.get_barrier_semaphore()
    for step in range(1, count):
        pl.semaphore_signal(
            barrier, inc=1, device_id={"hor": lax.rem(me + step, count)}, device_id_type=MESH
        )
    pl.semaphore_signal(barrier, inc=1, device_id={"dep": 1 - half}, device_id_type=MESH)

    def table_copy(kind, block):
        source = (table_high, table_low, back_high, back_low)[kind]
        target = (high_v, low_v, back_high_v, back_low_v)[kind]
        return pltpu.make_async_copy(
            source.at[block, pl.ds(0, target.shape[1])],
            target.at[block],
            table_sem.at[kind, block],
        )

    loads = [
        pltpu.make_async_copy(residual, res_v, load_sem.at[0]),
        pltpu.make_async_copy(bins, bins_v, load_sem.at[1]),
    ]
    late_loads = [
        pltpu.make_async_copy(classes, classes_v, load_sem.at[2]),
        pltpu.make_async_copy(
            table_high.at[0, pl.ds(x_cells, y_cells)], table_y_v, load_sem.at[3]
        ),
    ]
    blocks = [far, near, 2 + far, 2 + near]
    for load in loads:
        load.start()
    for block in blocks:
        table_copy(0, block).start()
        table_copy(1, block).start()
    for load in late_loads:
        load.start()

    lane = lax.broadcasted_iota(jnp.int32, (y_cells, width), 1)
    low_lanes = lane < width // 2

    def turn(value):
        return pltpu.roll(value, width // 2, 1)

    def mix(first, second):
        return (
            jnp.where(low_lanes, first, turn(second)),
            jnp.where(low_lanes, turn(first), second),
        )

    for load in loads:
        load.wait()
    focus_map = focus_base * jnp.exp(focus_step * bins_v[...].astype(jnp.float32))
    scaled = (focus_map * res_v[...]).reshape(rows, count * width)
    focus_v[...] = focus_map * (1.0 / (count * width * y_cells))
    high, low = split_values(scaled)
    stacked = jnp.concatenate([high, low], axis=0)

    def send_forward(chunk, target):
        return pltpu.make_async_remote_copy(
            src_ref=send_a.at[chunk, target],
            dst_ref=recv_a.at[chunk, me],
            send_sem=send_a_sem.at[chunk, target],
            recv_sem=recv_a_sem.at[chunk, me],
            device_id={"hor": target},
            device_id_type=MESH,
        )

    def wait_forward(chunk, source):
        pltpu.make_async_remote_copy(
            src_ref=send_a.at[chunk, source],
            dst_ref=recv_a.at[chunk, source],
            send_sem=send_a_sem.at[chunk, source],
            recv_sem=recv_a_sem.at[chunk, source],
            device_id={"hor": source},
            device_id_type=MESH,
        ).wait_recv()

    def send_back(chunk, target):
        return pltpu.make_async_remote_copy(
            src_ref=send_b.at[chunk, target],
            dst_ref=recv_b.at[chunk, me],
            send_sem=send_b_sem.at[chunk, target],
            recv_sem=recv_b_sem.at[chunk, me],
            device_id={"hor": target},
            device_id_type=MESH,
        )

    def wait_back(chunk, source):
        pltpu.make_async_remote_copy(
            src_ref=send_b.at[chunk, source],
            dst_ref=recv_b.at[chunk, source],
            send_sem=send_b_sem.at[chunk, source],
            recv_sem=recv_b_sem.at[chunk, source],
            device_id={"hor": source},
            device_id_type=MESH,
        ).wait_recv()

    far_targets = [4 * far + lax.rem(me + step, 4) for step in range(4)]
    near_targets = [4 * near + lax.rem(me + step, 4) for step in range(1, 4)]
    others = far_targets + near_targets

    for step, block in enumerate(blocks):
        chunk = step // 2
        side = far if step % 2 == 0 else near
        table_copy(0, block).wait()
        table_copy(1, block).wait()
        first = dot32(stacked, high_v[block])
        value = first[:rows] + first[rows:] + dot32(high, low_v[block])
        for pair in range(2):
            part = value[:, pair * width : (pair + 1) * width]
            even, odd = mix(part[: rows // 2], part[rows // 2 :])
            send_a[chunk, 4 * side + 2 * pair] = even.reshape(pairs, y_rows, width)
            send_a[chunk, 4 * side + 2 * pair + 1] = odd.reshape(pairs, y_rows, width)
        if step == 0:
            pl.semaphore_wait(barrier, count)
        if chunk == 0:
            for target in far_targets if step == 0 else near_targets:
                send_forward(0, target).start()
        if step % 2 == 1:
            recv_a[chunk, me] = send_a[chunk, me]

    for kind in (2, 3):
        for block in range(4):
            table_copy(kind, block).start()

    for load in late_loads:
        load.wait()
    for layer in range(2 * layers):
        index = jnp.full((8, width), classes_v[0, layer], jnp.int32).astype(jnp.float32)
        weights[layer] = weight_base * jnp.exp(weight_step * index)

    def layer_of(place):
        return place + half * (layers - 1 - 2 * place)

    def coupling_after(place):
        here = half * layers + layer_of(place)
        return coupling_scale * weights[here] * weights[here + 1 - 2 * half]

    def half_sines(frequency, length):
        sines = jnp.sin(frequency.astype(jnp.float32) * (math.pi / length))
        return 4.0 * sines * sines

    wave_x = half_sines(lax.broadcasted_iota(jnp.int32, (8, width), 1) + me * width, x_cells)
    row_index = lax.broadcasted_iota(jnp.int32, (y_cells, width), 0)
    wave_y = half_sines(row_index, y_cells).reshape(plane)
    wave = damping + smoothing * (wave_y + wave_x[None])

    def pivot_step(place, carried):
        here = weights[half * layers + layer_of(place)]
        excess = here[None] * wave + carried
        after = coupling_after(place)[None]
        reciprocal = 1.0 / (excess + after)
        inverse[layer_of(place)] = reciprocal
        scaled_after = after * reciprocal
        factor[layer_of(place)] = scaled_after
        edge_out[0] = excess
        return scaled_after * excess

    lax.fori_loop(0, layers, pivot_step, jnp.zeros(plane, jnp.float32))

    def edge_copy(slot):
        return pltpu.make_async_remote_copy(
            src_ref=edge_out.at[slot],
            dst_ref=edge_in.at[slot],
            send_sem=edge_send_sem.at[slot],
            recv_sem=edge_recv_sem.at[slot],
            device_id={"dep": 1 - half},
            device_id_type=MESH,
        )

    edge_copy(0).start()

    def response_step(step, following):
        place = layers - 2 - step
        value = factor[layer_of(place)] * following
        response[layer_of(place)] = value
        return value

    ones = jnp.ones(plane, jnp.float32)
    response[layer_of(layers - 1)] = ones
    lax.fori_loop(0, layers - 1, response_step, ones)

    def flat(value):
        return value.reshape(y_cells, width)

    def pack_step(row, carried):
        parts = mix(flat(inverse[row]), flat(inverse[row + pairs]))
        packed_inverse[0, row], packed_inverse[1, row] = (part.reshape(plane) for part in parts)
        parts = mix(flat(factor[row]), flat(factor[row + pairs]))
        packed_factor[0, row], packed_factor[1, row] = (part.reshape(plane) for part in parts)
        parts = mix(flat(response[row]), flat(response[row + pairs]))
        packed_response[0, row], packed_response[1, row] = (part.reshape(plane) for part in parts)
        return carried

    lax.fori_loop(0, pairs, pack_step, 0)

    edge_copy(0).wait()
    after = coupling_after(layers - 1)[None]
    here = edge_out[0]
    there = edge_in[0]
    scale = 1.0 / (here * there + after * (here + there))
    for target, value in ((gain_here, (there + after) * scale), (gain_there, after * scale)):
        parts = mix(flat(value), flat(value))
        target[0], target[1] = (part.reshape(plane) for part in parts)

    for target in others:
        send_forward(0, target).wait_send()
        send_forward(1, target).start()

    low_plane = low_lanes.reshape(plane)
    first_lanes = jnp.logical_xor(low_plane, jnp.full(plane, half, jnp.int32) == 1)

    def turn_plane(value):
        return turn(flat(value)).reshape(plane)

    def row_of(place):
        return place + half * (pairs - 1 - 2 * place)

    def transform_y(first, second):
        upper, lower = split_values(jnp.concatenate([first, second], axis=1))
        return dot32(table_y_v[...], jnp.concatenate([upper, upper, lower, lower], axis=0))

    for chunk in range(2):
        for source in others:
            wait_forward(chunk, source)
        for row in range(0, pairs, 2):
            value = transform_y(flat(recv_a[chunk, :, row]), flat(recv_a[chunk, :, row + 1]))
            spectrum[row] = value[:, :width].reshape(plane)
            spectrum[row + 1] = value[:, width:].reshape(plane)
        carried = jnp.zeros(plane, jnp.float32)
        for side in range(2):
            for place in range(pairs):
                row = row_of(place)
                value = spectrum[row] + carried
                spectrum[row] = value
                forwarded = packed_factor[chunk, row] * value
                carried = jnp.where(first_lanes, forwarded, 0.0)
                if side == 1:
                    carried = forwarded - carried
            carried = turn_plane(carried)
        edge_out[1 + chunk] = value
        edge_copy(1 + chunk).start()
        following = jnp.zeros(plane, jnp.float32)
        upper_part[row_of(pairs - 1)] = following
        for place in reversed(range(pairs - 1)):
            row = row_of(place)
            following = (
                packed_inverse[chunk, row] * spectrum[row] + packed_factor[chunk, row] * following
            )
            upper_part[row] = following
        following = turn_plane(following)
        for place in reversed(range(pairs)):
            row = row_of(place)
            following = (
                packed_inverse[chunk, row] * spectrum[row] + packed_factor[chunk, row] * following
            )
            spectrum[row] = jnp.where(first_lanes, following, upper_part[row])
        edge_copy(1 + chunk).wait()
        edge = gain_here[chunk] * value + gain_there[chunk] * turn_plane(edge_in[1 + chunk])
        edge = jnp.where(first_lanes, turn_plane(edge), edge)
        for row in range(0, pairs, 2):
            first = spectrum[row] + packed_response[chunk, row] * edge
            second = spectrum[row + 1] + packed_response[chunk, row + 1] * edge
            value = transform_y(flat(first), flat(second))
            send_b[chunk, :, row] = value[:, :width].reshape(count, y_rows, width)
            send_b[chunk, :, row + 1] = value[:, width:].reshape(count, y_rows, width)
        for target in others:
            send_back(chunk, target).start()
        recv_b[chunk, me] = send_b[chunk, me]

    for kind in (2, 3):
        for block in range(4):
            table_copy(kind, block).wait()

    def gathered(chunk, side):
        tops = []
        bottoms = []
        for pair in range(2):
            even = flat(recv_b[chunk, 4 * side + 2 * pair])
            odd = flat(recv_b[chunk, 4 * side + 2 * pair + 1])
            top, bottom = mix(even, odd)
            tops.append(top)
            bottoms.append(bottom)
        value = jnp.concatenate(
            [jnp.concatenate(tops, axis=1), jnp.concatenate(bottoms, axis=1)], axis=0
        )
        upper, lower = split_values(value)
        return jnp.concatenate([upper, lower], axis=0), upper

    def product(stacked, upper, block, columns):
        first = dot32(stacked, back_high_v[block, :, columns])
        return first[:rows] + first[rows:] + dot32(upper, back_low_v[block, :, columns])

    for step in range(4):
        chunk = step // 2
        side = near if step % 2 == 0 else far
        for source in near_targets if step % 2 == 0 else far_targets:
            wait_back(chunk, source)
        pieces = gathered(chunk, side)
        for index in range(count // 2):
            columns = slice(index * 2 * width, (index + 1) * 2 * width)
            total = product(*pieces, 2 * chunk + side, columns).reshape(layers, y_rows, 2 * width)
            if step > 0:
                total = total + result[:, :, columns]
            if step == 3:
                total = total * focus_v[:, :, columns]
            result[:, :, columns] = total

    for chunk in range(2):
        for target in others:
            if chunk == 1:
                send_forward(1, target).wait_send()
            send_back(chunk, target).wait_send()


def kernel_body(residual, focus_bins, layer_class):
    layers, y_rows, x_cells = residual.shape
    count = lax.axis_size("hor")
    width = x_cells // count
    y_cells = y_rows * count
    forward = []
    backward = []
    for table in split_table(x_cells):
        table = table.reshape(x_cells, count, 2, width // 2).transpose(2, 1, 3, 0)
        table = np.ascontiguousarray(table.reshape(4, 2 * width, x_cells))
        backward.append(table)
        forward.append(np.ascontiguousarray(table.transpose(0, 2, 1)))
    high_y, low_y = split_table(y_cells)
    table_y = np.concatenate([high_y, low_y, high_y, low_y], axis=1)
    filler = np.broadcast_to(table_y, (4,) + table_y.shape)
    forward[0] = np.concatenate([forward[0], filler], axis=1)
    pairs = layers // 2
    block = (2, count, pairs, y_rows, width)
    plane = (y_cells // 8, 8, width)
    f32, bf16, dma = jnp.float32, jnp.bfloat16, pltpu.SemaphoreType.DMA
    return pl.pallas_call(
        kernel,
        out_shape=jax.ShapeDtypeStruct(residual.shape, f32),
        in_specs=[pl.BlockSpec(memory_space=pl.ANY)] * 7,
        out_specs=pl.BlockSpec(memory_space=pltpu.VMEM),
        scratch_shapes=[
            pltpu.VMEM(residual.shape, f32),
            pltpu.VMEM(residual.shape, jnp.int32),
            pltpu.SMEM((1, 2 * layers), jnp.int32),
            pltpu.VMEM(table_y.shape, bf16),
            pltpu.VMEM(forward[1].shape, bf16),
            pltpu.VMEM(forward[1].shape, bf16),
            pltpu.VMEM(backward[0].shape, bf16),
            pltpu.VMEM(backward[1].shape, bf16),
            pltpu.VMEM(residual.shape, f32),
            pltpu.VMEM(block, f32),
            pltpu.VMEM(block, f32),
            pltpu.VMEM(block, f32),
            pltpu.VMEM(block, f32),
            pltpu.VMEM((2 * layers, 8, width), f32),
            pltpu.VMEM((layers,) + plane, f32),
            pltpu.VMEM((layers,) + plane, f32),
            pltpu.VMEM((2, pairs) + plane, f32),
            pltpu.VMEM((2, pairs) + plane, f32),
            pltpu.VMEM((layers,) + plane, f32),
            pltpu.VMEM((2, pairs) + plane, f32),
            pltpu.VMEM((pairs,) + plane, f32),
            pltpu.VMEM((pairs,) + plane, f32),
            pltpu.VMEM((2,) + plane, f32),
            pltpu.VMEM((2,) + plane, f32),
            pltpu.VMEM((3,) + plane, f32),
            pltpu.VMEM((3,) + plane, f32),
            dma((4,)),
            dma((4, 4)),
            dma((2, count)),
            dma((2, count)),
            dma((2, count)),
            dma((2, count)),
            dma((3,)),
            dma((3,)),
        ],
        compiler_params=pltpu.CompilerParams(
            collective_id=0, has_side_effects=True, vmem_limit_bytes=53 * 2**20
        ),
        cost_estimate=pl.CostEstimate(
            flops=2 * 6 * layers * y_rows * x_cells * x_cells,
            bytes_accessed=10 * 2**20,
            transcendentals=layers * y_rows * x_cells,
        ),
    )(
        residual,
        focus_bins,
        layer_class.reshape(1, -1),
        jnp.asarray(forward[0]),
        jnp.asarray(forward[1]),
        jnp.asarray(backward[0]),
        jnp.asarray(backward[1]),
    )


def fits_kernel(mesh):
    return mesh.shape["hor"] == 8 and mesh.shape["dep"] == 2


def chosen(mesh, residual, focus_bins, layer_class):
    shape = residual.shape
    if fits_kernel(mesh) and shape == (16, 8, 1024):
        return kernel_body(residual, focus_bins, layer_class)
    return body(residual, focus_bins, layer_class)


def solution(mesh):
    return jax.shard_map(
        functools.partial(chosen, mesh),
        mesh=mesh,
        in_specs=(P(("grp", "dep"), "hor", None), P(("grp", "dep"), "hor", None), P("grp")),
        out_specs=P(("grp", "dep"), "hor", None),
        check_vma=False,
    )
```

```python
import functools
import math

import jax
import jax.numpy as jnp
import ml_dtypes
import numpy as np
from jax import lax
from jax.experimental import pallas as pl
from jax.experimental.pallas import tpu as pltpu
from jax.sharding import PartitionSpec as P

damping = 0.01
smoothing = 1.0
coupling_scale = 1.0
weight_base = 0.5
weight_step = 0.2
focus_base = 0.5
focus_step = 0.09242
highest = lax.Precision.HIGHEST


def partner_2(value, axis, distance):
    mask = 2**distance
    pairs = [(source, source ^ mask) for source in range(lax.axis_size(axis))]
    return lax.ppermute(value, axis, pairs)


def depth_weights(layer_class):
    return weight_base * jnp.exp(weight_step * layer_class.astype(jnp.float32))


def focusing(focus_bins):
    return focus_base * jnp.exp(focus_step * focus_bins.astype(jnp.float32))


def couplings(weights):
    inner = coupling_scale * weights[:-1] * weights[1:]
    zero_end = jnp.zeros((1,), jnp.float32)
    return (jnp.concatenate([zero_end, inner]), jnp.concatenate([inner, zero_end]))


def symbol(frequency, length):
    return 2.0 - 2.0 * jnp.cos(frequency * (2.0 * math.pi / length))


def cas_table(length):
    position = jnp.arange(length, dtype=jnp.int32)
    product = position[:, None] * position[None, :] % length
    angles = product.astype(jnp.float32) * (2.0 * math.pi / length)
    return jnp.cos(angles) + jnp.sin(angles)


def shift_down(values, distance, fill_value):
    filler = jnp.full(values.shape[:-2] + (distance, values.shape[-1]), fill_value, values.dtype)
    return jnp.concatenate([filler, values[..., :-distance, :]], axis=-2)


def shift_up(values, distance, fill_value):
    filler = jnp.full(values.shape[:-2] + (distance, values.shape[-1]), fill_value, values.dtype)
    return jnp.concatenate([values[..., distance:, :], filler], axis=-2)


def reduce_step(lower, middle, upper, source, rows_below, rows_above):
    lower_below, middle_below, upper_below, source_below = rows_below
    lower_above, middle_above, upper_above, source_above = rows_above
    ratio_below = -lower / middle_below
    ratio_above = -upper / middle_above
    new_lower = ratio_below * lower_below
    new_middle = middle + ratio_below * upper_below + ratio_above * lower_above
    new_upper = ratio_above * upper_above
    new_source = source + ratio_below * source_below + ratio_above * source_above
    return (new_lower, new_middle, new_upper, new_source)


def local_solve(lower, middle, upper, source):
    layer_count = middle.shape[0]
    distance = 1
    while distance < layer_count:
        rows_below = (
            shift_down(lower, distance, 0.0),
            shift_down(middle, distance, 1.0),
            shift_down(upper, distance, 0.0),
            shift_down(source, distance, 0.0),
        )
        rows_above = (
            shift_up(lower, distance, 0.0),
            shift_up(middle, distance, 1.0),
            shift_up(upper, distance, 0.0),
            shift_up(source, distance, 0.0),
        )
        lower, middle, upper, source = reduce_step(
            lower, middle, upper, source, rows_below, rows_above
        )
        distance = distance * 2
    return source / middle


def body(residual, focus_bins, layer_class):
    depth_rows, y_rows, x_cells = residual.shape
    hor_count = lax.axis_size("hor")
    y_cells = y_rows * hor_count
    focus_map = focusing(focus_bins)
    scaled = focus_map * residual
    weights = depth_weights(layer_class)
    couple_prev, couple_next = couplings(weights)
    first_row = lax.axis_index("dep") * depth_rows
    table_x = cas_table(x_cells)
    table_y = cas_table(y_cells)
    symbol_y = symbol(jnp.arange(y_cells, dtype=jnp.float32), y_cells)
    block_width = x_cells // hor_count
    block_index = lax.axis_index("hor")
    spectra = jnp.einsum(
        "zcx,xbj->bzcj", scaled, table_x.reshape(x_cells, hor_count, block_width), precision=highest
    )
    spectra = spectra.reshape(hor_count, depth_rows, y_rows * block_width)
    table_rows = table_y.reshape(hor_count, y_rows, y_cells)
    portion = lax.all_to_all(spectra, "hor", split_axis=0, concat_axis=0, tiled=True)
    item_count = portion.shape[1]
    arranged = portion.reshape(hor_count, item_count, y_rows, block_width)
    spectrum = jnp.einsum("hzcj,hcy->zjy", arranged, table_rows, precision=highest)
    spectrum = spectrum.reshape(depth_rows, block_width * y_cells)
    wave_x = (block_index * block_width + jnp.arange(block_width, dtype=jnp.int32)).astype(
        jnp.float32
    )
    wave_term = (
        damping + smoothing * (symbol_y[None, :] + symbol(wave_x, x_cells)[:, None])
    ).reshape(-1)
    weight_local = lax.dynamic_slice_in_dim(weights, first_row, depth_rows)
    prev_local = lax.dynamic_slice_in_dim(couple_prev, first_row, depth_rows)
    next_local = lax.dynamic_slice_in_dim(couple_next, first_row, depth_rows)
    middle = weight_local[:, None] * wave_term[None, :] + (prev_local + next_local)[:, None]
    lower = jnp.broadcast_to(-prev_local[:, None], middle.shape)
    upper = jnp.broadcast_to(-next_local[:, None], middle.shape)
    row_index = jnp.arange(depth_rows, dtype=jnp.int32)
    edge_term = jnp.where(row_index == 0, prev_local[0], 0.0) + jnp.where(
        row_index == depth_rows - 1, next_local[depth_rows - 1], 0.0
    )
    source = jnp.stack([spectrum, jnp.broadcast_to(edge_term[:, None], spectrum.shape)])
    solutions = local_solve(lower, middle, upper, source)
    base_part = solutions[0]
    response = solutions[1]
    edge_row = (1 - lax.axis_index("dep")) * (depth_rows - 1)
    base_edge = lax.dynamic_index_in_dim(base_part, edge_row, 0, keepdims=False)
    response_edge = lax.dynamic_index_in_dim(response, edge_row, 0, keepdims=False)
    partner = partner_2(jnp.stack([base_edge, response_edge]), "dep", 0)
    divisor = 1.0 - response_edge * partner[1]
    interface = (partner[0] + partner[1] * base_edge) / divisor
    solved = base_part + response * interface[None, :]
    solved = solved.reshape(depth_rows, block_width, y_cells)
    returned = jnp.einsum(
        "zjk,khc->hzcj", solved, table_y.reshape(y_cells, hor_count, y_rows), precision=highest
    )
    returned = returned.reshape(hor_count, depth_rows, y_rows * block_width)
    table_back = table_x.reshape(hor_count, block_width, x_cells)
    portion = lax.all_to_all(returned, "hor", split_axis=0, concat_axis=0, tiled=True)
    item_count = portion.shape[1]
    arranged = portion.reshape(hor_count, item_count, y_rows, block_width)
    result_field = jnp.einsum("bzcj,bjx->zcx", arranged, table_back, precision=highest)
    return focus_map * result_field / (x_cells * y_cells)

MESH = pl.DeviceIdType.MESH


def split_table(length):
    position = np.arange(length)
    angles = (position[:, None] * position[None, :] % length) * (2.0 * math.pi / length)
    table = np.cos(angles) + np.sin(angles)
    high = table.astype(ml_dtypes.bfloat16)
    low = (table - high.astype(np.float64)).astype(ml_dtypes.bfloat16)
    return high, low


def split_values(values):
    high = values.astype(jnp.bfloat16)
    low = (values - high.astype(jnp.float32)).astype(jnp.bfloat16)
    return high, low


def dot32(left, right):
    return jnp.dot(left, right, preferred_element_type=jnp.float32)


def kernel(
    residual,
    bins,
    classes,
    table_high,
    table_low,
    back_high,
    back_low,
    result,
    res_v,
    bins_v,
    classes_v,
    table_y_v,
    high_v,
    low_v,
    back_high_v,
    back_low_v,
    focus_v,
    send_a,
    recv_a,
    send_b,
    recv_b,
    weights,
    inverse,
    factor,
    packed_inverse,
    packed_factor,
    response,
    packed_response,
    spectrum,
    upper_part,
    gain_here,
    gain_there,
    edge_out,
    edge_in,
    load_sem,
    table_sem,
    send_a_sem,
    recv_a_sem,
    send_b_sem,
    recv_b_sem,
    edge_send_sem,
    edge_recv_sem,
):
    _, count, pairs, y_rows, width = send_a.shape
    layers = 2 * pairs
    y_cells = count * y_rows
    plane = (y_cells // 8, 8, width)
    x_cells = count * width
    rows = layers * y_rows
    me = lax.axis_index("hor")
    half = lax.axis_index("dep")
    near = me // 4
    far = 1 - near

    barrier = pltpu.get_barrier_semaphore()
    for step in range(1, count):
        pl.semaphore_signal(
            barrier, inc=1, device_id={"hor": lax.rem(me + step, count)}, device_id_type=MESH
        )
    pl.semaphore_signal(barrier, inc=1, device_id={"dep": 1 - half}, device_id_type=MESH)

    def table_copy(kind, block):
        source = (table_high, table_low, back_high, back_low)[kind]
        target = (high_v, low_v, back_high_v, back_low_v)[kind]
        return pltpu.make_async_copy(
            source.at[block, pl.ds(0, target.shape[1])],
            target.at[block],
            table_sem.at[kind, block],
        )

    loads = [
        pltpu.make_async_copy(residual, res_v, load_sem.at[0]),
        pltpu.make_async_copy(bins, bins_v, load_sem.at[1]),
    ]
    late_loads = [
        pltpu.make_async_copy(classes, classes_v, load_sem.at[2]),
        pltpu.make_async_copy(
            table_high.at[0, pl.ds(x_cells, y_cells)], table_y_v, load_sem.at[3]
        ),
    ]
    blocks = [far, near, 2 + far, 2 + near]
    for load in loads:
        load.start()
    for block in blocks:
        table_copy(0, block).start()
        table_copy(1, block).start()
    for load in late_loads:
        load.start()

    lane = lax.broadcasted_iota(jnp.int32, (y_cells, width), 1)
    low_lanes = lane < width // 2

    def turn(value):
        return pltpu.roll(value, width // 2, 1)

    def mix(first, second):
        return (
            jnp.where(low_lanes, first, turn(second)),
            jnp.where(low_lanes, turn(first), second),
        )

    for load in loads:
        load.wait()
    focus_map = focus_base * jnp.exp(focus_step * bins_v[...].astype(jnp.float32))
    scaled = (focus_map * res_v[...]).reshape(rows, count * width)
    focus_v[...] = focus_map * (1.0 / (count * width * y_cells))
    high, low = split_values(scaled)
    stacked = jnp.concatenate([high, low], axis=0)

    def send_forward(chunk, target):
        return pltpu.make_async_remote_copy(
            src_ref=send_a.at[chunk, target],
            dst_ref=recv_a.at[chunk, me],
            send_sem=send_a_sem.at[chunk, target],
            recv_sem=recv_a_sem.at[chunk, me],
            device_id={"hor": target},
            device_id_type=MESH,
        )

    def wait_forward(chunk, source):
        pltpu.make_async_remote_copy(
            src_ref=send_a.at[chunk, source],
            dst_ref=recv_a.at[chunk, source],
            send_sem=send_a_sem.at[chunk, source],
            recv_sem=recv_a_sem.at[chunk, source],
            device_id={"hor": source},
            device_id_type=MESH,
        ).wait_recv()

    def send_back(chunk, target):
        return pltpu.make_async_remote_copy(
            src_ref=send_b.at[chunk, target],
            dst_ref=recv_b.at[chunk, me],
            send_sem=send_b_sem.at[chunk, target],
            recv_sem=recv_b_sem.at[chunk, me],
            device_id={"hor": target},
            device_id_type=MESH,
        )

    def wait_back(chunk, source):
        pltpu.make_async_remote_copy(
            src_ref=send_b.at[chunk, source],
            dst_ref=recv_b.at[chunk, source],
            send_sem=send_b_sem.at[chunk, source],
            recv_sem=recv_b_sem.at[chunk, source],
            device_id={"hor": source},
            device_id_type=MESH,
        ).wait_recv()

    far_targets = [4 * far + lax.rem(me + step, 4) for step in range(4)]
    near_targets = [4 * near + lax.rem(me + step, 4) for step in range(1, 4)]
    others = far_targets + near_targets

    for step, block in enumerate(blocks):
        chunk = step // 2
        side = far if step % 2 == 0 else near
        table_copy(0, block).wait()
        table_copy(1, block).wait()
        first = dot32(stacked, high_v[block])
        value = first[:rows] + first[rows:] + dot32(high, low_v[block])
        for pair in range(2):
            part = value[:, pair * width : (pair + 1) * width]
            even, odd = mix(part[: rows // 2], part[rows // 2 :])
            send_a[chunk, 4 * side + 2 * pair] = even.reshape(pairs, y_rows, width)
            send_a[chunk, 4 * side + 2 * pair + 1] = odd.reshape(pairs, y_rows, width)
        if step == 0:
            pl.semaphore_wait(barrier, count)
        targets = far_targets if step % 2 == 0 else near_targets
        for target in targets[:1] if step == 2 else targets:
            send_forward(chunk, target).start()
        if step % 2 == 1:
            recv_a[chunk, me] = send_a[chunk, me]

    for kind in (2, 3):
        for block in range(4):
            table_copy(kind, block).start()

    for load in late_loads:
        load.wait()
    for layer in range(2 * layers):
        index = jnp.full((8, width), classes_v[0, layer], jnp.int32).astype(jnp.float32)
        weights[layer] = weight_base * jnp.exp(weight_step * index)

    def layer_of(place):
        return place + half * (layers - 1 - 2 * place)

    def coupling_after(place):
        here = half * layers + layer_of(place)
        return coupling_scale * weights[here] * weights[here + 1 - 2 * half]

    def half_sines(frequency, length):
        sines = jnp.sin(frequency.astype(jnp.float32) * (math.pi / length))
        return 4.0 * sines * sines

    wave_x = half_sines(lax.broadcasted_iota(jnp.int32, (8, width), 1) + me * width, x_cells)
    row_index = lax.broadcasted_iota(jnp.int32, (y_cells, width), 0)
    wave_y = half_sines(row_index, y_cells).reshape(plane)
    wave = damping + smoothing * (wave_y + wave_x[None])

    def pivot_step(place, carried):
        here = weights[half * layers + layer_of(place)]
        excess = here[None] * wave + carried
        after = coupling_after(place)[None]
        reciprocal = 1.0 / (excess + after)
        inverse[layer_of(place)] = reciprocal
        scaled_after = after * reciprocal
        factor[layer_of(place)] = scaled_after
        edge_out[0] = excess
        return scaled_after * excess

    lax.fori_loop(0, layers, pivot_step, jnp.zeros(plane, jnp.float32))

    def edge_copy(slot):
        return pltpu.make_async_remote_copy(
            src_ref=edge_out.at[slot],
            dst_ref=edge_in.at[slot],
            send_sem=edge_send_sem.at[slot],
            recv_sem=edge_recv_sem.at[slot],
            device_id={"dep": 1 - half},
            device_id_type=MESH,
        )

    edge_copy(0).start()

    def response_step(step, following):
        place = layers - 2 - step
        value = factor[layer_of(place)] * following
        response[layer_of(place)] = value
        return value

    ones = jnp.ones(plane, jnp.float32)
    response[layer_of(layers - 1)] = ones
    lax.fori_loop(0, layers - 1, response_step, ones)

    def flat(value):
        return value.reshape(y_cells, width)

    def pack_step(row, carried):
        parts = mix(flat(inverse[row]), flat(inverse[row + pairs]))
        packed_inverse[0, row], packed_inverse[1, row] = (part.reshape(plane) for part in parts)
        parts = mix(flat(factor[row]), flat(factor[row + pairs]))
        packed_factor[0, row], packed_factor[1, row] = (part.reshape(plane) for part in parts)
        parts = mix(flat(response[row]), flat(response[row + pairs]))
        packed_response[0, row], packed_response[1, row] = (part.reshape(plane) for part in parts)
        return carried

    lax.fori_loop(0, pairs, pack_step, 0)

    edge_copy(0).wait()
    after = coupling_after(layers - 1)[None]
    here = edge_out[0]
    there = edge_in[0]
    scale = 1.0 / (here * there + after * (here + there))
    for target, value in ((gain_here, (there + after) * scale), (gain_there, after * scale)):
        parts = mix(flat(value), flat(value))
        target[0], target[1] = (part.reshape(plane) for part in parts)

    for first, second in zip(far_targets[:3], far_targets[1:]):
        send_forward(0, first).wait_send()
        send_forward(1, second).start()

    low_plane = low_lanes.reshape(plane)
    first_lanes = jnp.logical_xor(low_plane, jnp.full(plane, half, jnp.int32) == 1)

    def turn_plane(value):
        return turn(flat(value)).reshape(plane)

    def row_of(place):
        return place + half * (pairs - 1 - 2 * place)

    def transform_y(first, second):
        upper, lower = split_values(jnp.concatenate([first, second], axis=1))
        return dot32(table_y_v[...], jnp.concatenate([upper, upper, lower, lower], axis=0))

    for chunk in range(2):
        for source in others:
            wait_forward(chunk, source)
        for row in range(0, pairs, 2):
            value = transform_y(flat(recv_a[chunk, :, row]), flat(recv_a[chunk, :, row + 1]))
            spectrum[row] = value[:, :width].reshape(plane)
            spectrum[row + 1] = value[:, width:].reshape(plane)
        carried = jnp.zeros(plane, jnp.float32)
        for side in range(2):
            for place in range(pairs):
                row = row_of(place)
                value = spectrum[row] + carried
                spectrum[row] = value
                forwarded = packed_factor[chunk, row] * value
                carried = jnp.where(first_lanes, forwarded, 0.0)
                if side == 1:
                    carried = forwarded - carried
            carried = turn_plane(carried)
        edge_out[1 + chunk] = value
        edge_copy(1 + chunk).start()
        following = jnp.zeros(plane, jnp.float32)
        upper_part[row_of(pairs - 1)] = following
        for place in reversed(range(pairs - 1)):
            row = row_of(place)
            following = (
                packed_inverse[chunk, row] * spectrum[row] + packed_factor[chunk, row] * following
            )
            upper_part[row] = following
        following = turn_plane(following)
        for place in reversed(range(pairs)):
            row = row_of(place)
            following = (
                packed_inverse[chunk, row] * spectrum[row] + packed_factor[chunk, row] * following
            )
            spectrum[row] = jnp.where(first_lanes, following, upper_part[row])
        edge_copy(1 + chunk).wait()
        edge = gain_here[chunk] * value + gain_there[chunk] * turn_plane(edge_in[1 + chunk])
        edge = jnp.where(first_lanes, turn_plane(edge), edge)
        for row in range(0, pairs, 2):
            first = spectrum[row] + packed_response[chunk, row] * edge
            second = spectrum[row + 1] + packed_response[chunk, row + 1] * edge
            value = transform_y(flat(first), flat(second))
            send_b[chunk, :, row] = value[:, :width].reshape(count, y_rows, width)
            send_b[chunk, :, row + 1] = value[:, width:].reshape(count, y_rows, width)
        for target in others:
            send_back(chunk, target).start()
        recv_b[chunk, me] = send_b[chunk, me]

    for kind in (2, 3):
        for block in range(4):
            table_copy(kind, block).wait()

    def gathered(chunk, side):
        tops = []
        bottoms = []
        for pair in range(2):
            even = flat(recv_b[chunk, 4 * side + 2 * pair])
            odd = flat(recv_b[chunk, 4 * side + 2 * pair + 1])
            top, bottom = mix(even, odd)
            tops.append(top)
            bottoms.append(bottom)
        value = jnp.concatenate(
            [jnp.concatenate(tops, axis=1), jnp.concatenate(bottoms, axis=1)], axis=0
        )
        upper, lower = split_values(value)
        return jnp.concatenate([upper, lower], axis=0), upper

    def product(stacked, upper, block, columns):
        first = dot32(stacked, back_high_v[block, :, columns])
        return first[:rows] + first[rows:] + dot32(upper, back_low_v[block, :, columns])

    for step in range(4):
        chunk = step // 2
        side = near if step % 2 == 0 else far
        for source in near_targets if step % 2 == 0 else far_targets:
            wait_back(chunk, source)
        pieces = gathered(chunk, side)
        for index in range(count // 2):
            columns = slice(index * 2 * width, (index + 1) * 2 * width)
            total = product(*pieces, 2 * chunk + side, columns).reshape(layers, y_rows, 2 * width)
            if step > 0:
                total = total + result[:, :, columns]
            if step == 3:
                total = total * focus_v[:, :, columns]
            result[:, :, columns] = total

    for place, target in enumerate(others):
        if place > 2:
            send_forward(0, target).wait_send()
        send_forward(1, target).wait_send()
        send_back(0, target).wait_send()
        send_back(1, target).wait_send()


def kernel_body(residual, focus_bins, layer_class):
    layers, y_rows, x_cells = residual.shape
    count = lax.axis_size("hor")
    width = x_cells // count
    y_cells = y_rows * count
    forward = []
    backward = []
    for table in split_table(x_cells):
        table = table.reshape(x_cells, count, 2, width // 2).transpose(2, 1, 3, 0)
        table = np.ascontiguousarray(table.reshape(4, 2 * width, x_cells))
        backward.append(table)
        forward.append(np.ascontiguousarray(table.transpose(0, 2, 1)))
    high_y, low_y = split_table(y_cells)
    table_y = np.concatenate([high_y, low_y, high_y, low_y], axis=1)
    filler = np.broadcast_to(table_y, (4,) + table_y.shape)
    forward[0] = np.concatenate([forward[0], filler], axis=1)
    pairs = layers // 2
    block = (2, count, pairs, y_rows, width)
    plane = (y_cells // 8, 8, width)
    f32, bf16, dma = jnp.float32, jnp.bfloat16, pltpu.SemaphoreType.DMA
    return pl.pallas_call(
        kernel,
        out_shape=jax.ShapeDtypeStruct(residual.shape, f32),
        in_specs=[pl.BlockSpec(memory_space=pl.ANY)] * 7,
        out_specs=pl.BlockSpec(memory_space=pltpu.VMEM),
        scratch_shapes=[
            pltpu.VMEM(residual.shape, f32),
            pltpu.VMEM(residual.shape, jnp.int32),
            pltpu.SMEM((1, 2 * layers), jnp.int32),
            pltpu.VMEM(table_y.shape, bf16),
            pltpu.VMEM(forward[1].shape, bf16),
            pltpu.VMEM(forward[1].shape, bf16),
            pltpu.VMEM(backward[0].shape, bf16),
            pltpu.VMEM(backward[1].shape, bf16),
            pltpu.VMEM(residual.shape, f32),
            pltpu.VMEM(block, f32),
            pltpu.VMEM(block, f32),
            pltpu.VMEM(block, f32),
            pltpu.VMEM(block, f32),
            pltpu.VMEM((2 * layers, 8, width), f32),
            pltpu.VMEM((layers,) + plane, f32),
            pltpu.VMEM((layers,) + plane, f32),
            pltpu.VMEM((2, pairs) + plane, f32),
            pltpu.VMEM((2, pairs) + plane, f32),
            pltpu.VMEM((layers,) + plane, f32),
            pltpu.VMEM((2, pairs) + plane, f32),
            pltpu.VMEM((pairs,) + plane, f32),
            pltpu.VMEM((pairs,) + plane, f32),
            pltpu.VMEM((2,) + plane, f32),
            pltpu.VMEM((2,) + plane, f32),
            pltpu.VMEM((3,) + plane, f32),
            pltpu.VMEM((3,) + plane, f32),
            dma((4,)),
            dma((4, 4)),
            dma((2, count)),
            dma((2, count)),
            dma((2, count)),
            dma((2, count)),
            dma((3,)),
            dma((3,)),
        ],
        compiler_params=pltpu.CompilerParams(
            collective_id=0, has_side_effects=True, vmem_limit_bytes=54716 * 2**10
        ),
        cost_estimate=pl.CostEstimate(
            flops=2 * 6 * layers * y_rows * x_cells * x_cells,
            bytes_accessed=10 * 2**20,
            transcendentals=layers * y_rows * x_cells,
        ),
    )(
        residual,
        focus_bins,
        layer_class.reshape(1, -1),
        jnp.asarray(forward[0]),
        jnp.asarray(forward[1]),
        jnp.asarray(backward[0]),
        jnp.asarray(backward[1]),
    )


def fits_kernel(mesh):
    return mesh.shape["hor"] == 8 and mesh.shape["dep"] == 2


def chosen(mesh, residual, focus_bins, layer_class):
    shape = residual.shape
    if fits_kernel(mesh) and shape == (16, 8, 1024):
        return kernel_body(residual, focus_bins, layer_class)
    return body(residual, focus_bins, layer_class)


def solution(mesh):
    return jax.shard_map(
        functools.partial(chosen, mesh),
        mesh=mesh,
        in_specs=(P(("grp", "dep"), "hor", None), P(("grp", "dep"), "hor", None), P("grp")),
        out_specs=P(("grp", "dep"), "hor", None),
        check_vma=False,
    )
```

```python
import functools
import math

import jax
import jax.numpy as jnp
import ml_dtypes
import numpy as np
from jax import lax
from jax.experimental import pallas as pl
from jax.experimental.pallas import tpu as pltpu
from jax.sharding import PartitionSpec as P

damping = 0.01
smoothing = 1.0
coupling_scale = 1.0
weight_base = 0.5
weight_step = 0.2
focus_base = 0.5
focus_step = 0.09242
highest = lax.Precision.HIGHEST


def partner_2(value, axis, distance):
    mask = 2**distance
    pairs = [(source, source ^ mask) for source in range(lax.axis_size(axis))]
    return lax.ppermute(value, axis, pairs)


def depth_weights(layer_class):
    return weight_base * jnp.exp(weight_step * layer_class.astype(jnp.float32))


def focusing(focus_bins):
    return focus_base * jnp.exp(focus_step * focus_bins.astype(jnp.float32))


def couplings(weights):
    inner = coupling_scale * weights[:-1] * weights[1:]
    zero_end = jnp.zeros((1,), jnp.float32)
    return (jnp.concatenate([zero_end, inner]), jnp.concatenate([inner, zero_end]))


def symbol(frequency, length):
    return 2.0 - 2.0 * jnp.cos(frequency * (2.0 * math.pi / length))


def cas_table(length):
    position = jnp.arange(length, dtype=jnp.int32)
    product = position[:, None] * position[None, :] % length
    angles = product.astype(jnp.float32) * (2.0 * math.pi / length)
    return jnp.cos(angles) + jnp.sin(angles)


def shift_down(values, distance, fill_value):
    filler = jnp.full(values.shape[:-2] + (distance, values.shape[-1]), fill_value, values.dtype)
    return jnp.concatenate([filler, values[..., :-distance, :]], axis=-2)


def shift_up(values, distance, fill_value):
    filler = jnp.full(values.shape[:-2] + (distance, values.shape[-1]), fill_value, values.dtype)
    return jnp.concatenate([values[..., distance:, :], filler], axis=-2)


def reduce_step(lower, middle, upper, source, rows_below, rows_above):
    lower_below, middle_below, upper_below, source_below = rows_below
    lower_above, middle_above, upper_above, source_above = rows_above
    ratio_below = -lower / middle_below
    ratio_above = -upper / middle_above
    new_lower = ratio_below * lower_below
    new_middle = middle + ratio_below * upper_below + ratio_above * lower_above
    new_upper = ratio_above * upper_above
    new_source = source + ratio_below * source_below + ratio_above * source_above
    return (new_lower, new_middle, new_upper, new_source)


def local_solve(lower, middle, upper, source):
    layer_count = middle.shape[0]
    distance = 1
    while distance < layer_count:
        rows_below = (
            shift_down(lower, distance, 0.0),
            shift_down(middle, distance, 1.0),
            shift_down(upper, distance, 0.0),
            shift_down(source, distance, 0.0),
        )
        rows_above = (
            shift_up(lower, distance, 0.0),
            shift_up(middle, distance, 1.0),
            shift_up(upper, distance, 0.0),
            shift_up(source, distance, 0.0),
        )
        lower, middle, upper, source = reduce_step(
            lower, middle, upper, source, rows_below, rows_above
        )
        distance = distance * 2
    return source / middle


def body(residual, focus_bins, layer_class):
    depth_rows, y_rows, x_cells = residual.shape
    hor_count = lax.axis_size("hor")
    y_cells = y_rows * hor_count
    focus_map = focusing(focus_bins)
    scaled = focus_map * residual
    weights = depth_weights(layer_class)
    couple_prev, couple_next = couplings(weights)
    first_row = lax.axis_index("dep") * depth_rows
    table_x = cas_table(x_cells)
    table_y = cas_table(y_cells)
    symbol_y = symbol(jnp.arange(y_cells, dtype=jnp.float32), y_cells)
    block_width = x_cells // hor_count
    block_index = lax.axis_index("hor")
    spectra = jnp.einsum(
        "zcx,xbj->bzcj", scaled, table_x.reshape(x_cells, hor_count, block_width), precision=highest
    )
    spectra = spectra.reshape(hor_count, depth_rows, y_rows * block_width)
    table_rows = table_y.reshape(hor_count, y_rows, y_cells)
    portion = lax.all_to_all(spectra, "hor", split_axis=0, concat_axis=0, tiled=True)
    item_count = portion.shape[1]
    arranged = portion.reshape(hor_count, item_count, y_rows, block_width)
    spectrum = jnp.einsum("hzcj,hcy->zjy", arranged, table_rows, precision=highest)
    spectrum = spectrum.reshape(depth_rows, block_width * y_cells)
    wave_x = (block_index * block_width + jnp.arange(block_width, dtype=jnp.int32)).astype(
        jnp.float32
    )
    wave_term = (
        damping + smoothing * (symbol_y[None, :] + symbol(wave_x, x_cells)[:, None])
    ).reshape(-1)
    weight_local = lax.dynamic_slice_in_dim(weights, first_row, depth_rows)
    prev_local = lax.dynamic_slice_in_dim(couple_prev, first_row, depth_rows)
    next_local = lax.dynamic_slice_in_dim(couple_next, first_row, depth_rows)
    middle = weight_local[:, None] * wave_term[None, :] + (prev_local + next_local)[:, None]
    lower = jnp.broadcast_to(-prev_local[:, None], middle.shape)
    upper = jnp.broadcast_to(-next_local[:, None], middle.shape)
    row_index = jnp.arange(depth_rows, dtype=jnp.int32)
    edge_term = jnp.where(row_index == 0, prev_local[0], 0.0) + jnp.where(
        row_index == depth_rows - 1, next_local[depth_rows - 1], 0.0
    )
    source = jnp.stack([spectrum, jnp.broadcast_to(edge_term[:, None], spectrum.shape)])
    solutions = local_solve(lower, middle, upper, source)
    base_part = solutions[0]
    response = solutions[1]
    edge_row = (1 - lax.axis_index("dep")) * (depth_rows - 1)
    base_edge = lax.dynamic_index_in_dim(base_part, edge_row, 0, keepdims=False)
    response_edge = lax.dynamic_index_in_dim(response, edge_row, 0, keepdims=False)
    partner = partner_2(jnp.stack([base_edge, response_edge]), "dep", 0)
    divisor = 1.0 - response_edge * partner[1]
    interface = (partner[0] + partner[1] * base_edge) / divisor
    solved = base_part + response * interface[None, :]
    solved = solved.reshape(depth_rows, block_width, y_cells)
    returned = jnp.einsum(
        "zjk,khc->hzcj", solved, table_y.reshape(y_cells, hor_count, y_rows), precision=highest
    )
    returned = returned.reshape(hor_count, depth_rows, y_rows * block_width)
    table_back = table_x.reshape(hor_count, block_width, x_cells)
    portion = lax.all_to_all(returned, "hor", split_axis=0, concat_axis=0, tiled=True)
    item_count = portion.shape[1]
    arranged = portion.reshape(hor_count, item_count, y_rows, block_width)
    result_field = jnp.einsum("bzcj,bjx->zcx", arranged, table_back, precision=highest)
    return focus_map * result_field / (x_cells * y_cells)

MESH = pl.DeviceIdType.MESH


def split_table(length):
    position = np.arange(length)
    angles = (position[:, None] * position[None, :] % length) * (2.0 * math.pi / length)
    table = np.cos(angles) + np.sin(angles)
    high = table.astype(ml_dtypes.bfloat16)
    low = (table - high.astype(np.float64)).astype(ml_dtypes.bfloat16)
    return high, low


def split_values(values):
    high = values.astype(jnp.bfloat16)
    low = (values - high.astype(jnp.float32)).astype(jnp.bfloat16)
    return high, low


def dot32(left, right):
    return jnp.dot(left, right, preferred_element_type=jnp.float32)


def kernel(
    residual,
    bins,
    classes,
    table_high,
    table_low,
    back_high,
    back_low,
    result,
    res_v,
    bins_v,
    classes_v,
    table_y_v,
    high_v,
    low_v,
    back_high_v,
    back_low_v,
    focus_v,
    send_a,
    recv_a,
    send_b,
    recv_b,
    weights,
    inverse,
    factor,
    packed_inverse,
    packed_factor,
    response,
    packed_response,
    spectrum,
    upper_part,
    gain_here,
    gain_there,
    edge_out,
    edge_in,
    load_sem,
    table_sem,
    send_a_sem,
    recv_a_sem,
    send_b_sem,
    recv_b_sem,
    edge_send_sem,
    edge_recv_sem,
):
    _, count, pairs, y_rows, width = send_a.shape
    layers = 2 * pairs
    y_cells = count * y_rows
    plane = (y_cells // 8, 8, width)
    x_cells = count * width
    rows = layers * y_rows
    me = lax.axis_index("hor")
    half = lax.axis_index("dep")
    near = me // 4
    far = 1 - near

    def table_copy(kind, block):
        source = (table_high, table_low, back_high, back_low)[kind]
        target = (high_v, low_v, back_high_v, back_low_v)[kind]
        return pltpu.make_async_copy(
            source.at[block, pl.ds(0, target.shape[1])],
            target.at[block],
            table_sem.at[kind, block],
        )

    loads = [
        pltpu.make_async_copy(residual, res_v, load_sem.at[0]),
        pltpu.make_async_copy(bins, bins_v, load_sem.at[1]),
    ]
    late_loads = [
        pltpu.make_async_copy(classes, classes_v, load_sem.at[2]),
        pltpu.make_async_copy(
            table_high.at[0, pl.ds(x_cells, y_cells)], table_y_v, load_sem.at[3]
        ),
    ]
    blocks = [far, near, 2 + far, 2 + near]
    for load in loads:
        load.start()
    for kind in range(2):
        table_copy(kind, far).start()

    barrier = pltpu.get_barrier_semaphore()
    for step in range(1, count):
        pl.semaphore_signal(
            barrier, inc=1, device_id={"hor": lax.rem(me + step, count)}, device_id_type=MESH
        )
    pl.semaphore_signal(barrier, inc=1, device_id={"dep": 1 - half}, device_id_type=MESH)

    for block in blocks[1:]:
        table_copy(0, block).start()
        table_copy(1, block).start()
    for load in late_loads:
        load.start()

    lane = lax.broadcasted_iota(jnp.int32, (y_cells, width), 1)
    low_lanes = lane < width // 2

    def turn(value):
        return pltpu.roll(value, width // 2, 1)

    def mix(first, second):
        return (
            jnp.where(low_lanes, first, turn(second)),
            jnp.where(low_lanes, turn(first), second),
        )

    for load in loads:
        load.wait()
    focus_map = focus_base * jnp.exp(focus_step * bins_v[...].astype(jnp.float32))
    scaled = (focus_map * res_v[...]).reshape(rows, count * width)
    focus_v[...] = focus_map * (1.0 / (count * width * y_cells))
    high, low = split_values(scaled)
    stacked = jnp.concatenate([high, low], axis=0)

    def send_forward(chunk, target):
        return pltpu.make_async_remote_copy(
            src_ref=send_a.at[chunk, target],
            dst_ref=recv_a.at[chunk, me],
            send_sem=send_a_sem.at[chunk, target],
            recv_sem=recv_a_sem.at[chunk, me],
            device_id={"hor": target},
            device_id_type=MESH,
        )

    def wait_forward(chunk, source):
        pltpu.make_async_remote_copy(
            src_ref=send_a.at[chunk, source],
            dst_ref=recv_a.at[chunk, source],
            send_sem=send_a_sem.at[chunk, source],
            recv_sem=recv_a_sem.at[chunk, source],
            device_id={"hor": source},
            device_id_type=MESH,
        ).wait_recv()

    def send_back(chunk, target):
        return pltpu.make_async_remote_copy(
            src_ref=send_b.at[chunk, target],
            dst_ref=recv_b.at[chunk, me],
            send_sem=send_b_sem.at[chunk, target],
            recv_sem=recv_b_sem.at[chunk, me],
            device_id={"hor": target},
            device_id_type=MESH,
        )

    def wait_back(chunk, source):
        pltpu.make_async_remote_copy(
            src_ref=send_b.at[chunk, source],
            dst_ref=recv_b.at[chunk, source],
            send_sem=send_b_sem.at[chunk, source],
            recv_sem=recv_b_sem.at[chunk, source],
            device_id={"hor": source},
            device_id_type=MESH,
        ).wait_recv()

    far_targets = [4 * far + lax.rem(me + step, 4) for step in range(4)]
    near_targets = [4 * near + lax.rem(me + step, 4) for step in range(1, 4)]
    others = far_targets + near_targets

    for step, block in enumerate(blocks):
        chunk = step // 2
        side = far if step % 2 == 0 else near
        table_copy(0, block).wait()
        table_copy(1, block).wait()
        first = dot32(stacked, high_v[block])
        value = first[:rows] + first[rows:] + dot32(high, low_v[block])
        for pair in range(2):
            part = value[:, pair * width : (pair + 1) * width]
            even, odd = mix(part[: rows // 2], part[rows // 2 :])
            send_a[chunk, 4 * side + 2 * pair] = even.reshape(pairs, y_rows, width)
            send_a[chunk, 4 * side + 2 * pair + 1] = odd.reshape(pairs, y_rows, width)
        if step == 0:
            pl.semaphore_wait(barrier, count)
        targets = far_targets if step % 2 == 0 else near_targets
        for target in targets[:1] if step == 2 else targets:
            send_forward(chunk, target).start()
        if step % 2 == 1:
            recv_a[chunk, me] = send_a[chunk, me]

    for kind in (2, 3):
        for block in range(4):
            table_copy(kind, block).start()

    for load in late_loads:
        load.wait()
    for layer in range(2 * layers):
        index = jnp.full((8, width), classes_v[0, layer], jnp.int32).astype(jnp.float32)
        weights[layer] = weight_base * jnp.exp(weight_step * index)

    def layer_of(place):
        return place + half * (layers - 1 - 2 * place)

    def coupling_after(place):
        here = half * layers + layer_of(place)
        return coupling_scale * weights[here] * weights[here + 1 - 2 * half]

    def half_sines(frequency, length):
        sines = jnp.sin(frequency.astype(jnp.float32) * (math.pi / length))
        return 4.0 * sines * sines

    wave_x = half_sines(lax.broadcasted_iota(jnp.int32, (8, width), 1) + me * width, x_cells)
    row_index = lax.broadcasted_iota(jnp.int32, (y_cells, width), 0)
    wave_y = half_sines(row_index, y_cells).reshape(plane)
    wave = damping + smoothing * (wave_y + wave_x[None])

    def pivot_step(place, carried):
        here = weights[half * layers + layer_of(place)]
        excess = here[None] * wave + carried
        after = coupling_after(place)[None]
        reciprocal = 1.0 / (excess + after)
        inverse[layer_of(place)] = reciprocal
        scaled_after = after * reciprocal
        factor[layer_of(place)] = scaled_after
        edge_out[0] = excess
        return scaled_after * excess

    lax.fori_loop(0, layers, pivot_step, jnp.zeros(plane, jnp.float32))

    def edge_copy(slot):
        return pltpu.make_async_remote_copy(
            src_ref=edge_out.at[slot],
            dst_ref=edge_in.at[slot],
            send_sem=edge_send_sem.at[slot],
            recv_sem=edge_recv_sem.at[slot],
            device_id={"dep": 1 - half},
            device_id_type=MESH,
        )

    edge_copy(0).start()

    def response_step(step, following):
        place = layers - 2 - step
        value = factor[layer_of(place)] * following
        response[layer_of(place)] = value
        return value

    ones = jnp.ones(plane, jnp.float32)
    response[layer_of(layers - 1)] = ones
    lax.fori_loop(0, layers - 1, response_step, ones)

    def flat(value):
        return value.reshape(y_cells, width)

    def pack_step(row, carried):
        parts = mix(flat(inverse[row]), flat(inverse[row + pairs]))
        packed_inverse[0, row], packed_inverse[1, row] = (part.reshape(plane) for part in parts)
        parts = mix(flat(factor[row]), flat(factor[row + pairs]))
        packed_factor[0, row], packed_factor[1, row] = (part.reshape(plane) for part in parts)
        parts = mix(flat(response[row]), flat(response[row + pairs]))
        packed_response[0, row], packed_response[1, row] = (part.reshape(plane) for part in parts)
        return carried

    lax.fori_loop(0, pairs, pack_step, 0)

    edge_copy(0).wait()
    after = coupling_after(layers - 1)[None]
    here = edge_out[0]
    there = edge_in[0]
    scale = 1.0 / (here * there + after * (here + there))
    for target, value in ((gain_here, (there + after) * scale), (gain_there, after * scale)):
        parts = mix(flat(value), flat(value))
        target[0], target[1] = (part.reshape(plane) for part in parts)

    for first, second in zip(far_targets[:3], far_targets[1:]):
        send_forward(0, first).wait_send()
        send_forward(1, second).start()

    low_plane = low_lanes.reshape(plane)
    first_lanes = jnp.logical_xor(low_plane, jnp.full(plane, half, jnp.int32) == 1)

    def turn_plane(value):
        return turn(flat(value)).reshape(plane)

    def row_of(place):
        return place + half * (pairs - 1 - 2 * place)

    def transform_y(first, second):
        upper, lower = split_values(jnp.concatenate([first, second], axis=1))
        return dot32(table_y_v[...], jnp.concatenate([upper, upper, lower, lower], axis=0))

    for chunk in range(2):
        for source in others:
            wait_forward(chunk, source)
        for row in range(0, pairs, 2):
            value = transform_y(flat(recv_a[chunk, :, row]), flat(recv_a[chunk, :, row + 1]))
            spectrum[row] = value[:, :width].reshape(plane)
            spectrum[row + 1] = value[:, width:].reshape(plane)
        carried = jnp.zeros(plane, jnp.float32)
        for side in range(2):
            for place in range(pairs):
                row = row_of(place)
                value = spectrum[row] + carried
                spectrum[row] = value
                forwarded = packed_factor[chunk, row] * value
                carried = jnp.where(first_lanes, forwarded, 0.0)
                if side == 1:
                    carried = forwarded - carried
            carried = turn_plane(carried)
        edge_out[1 + chunk] = value
        edge_copy(1 + chunk).start()
        following = jnp.zeros(plane, jnp.float32)
        upper_part[row_of(pairs - 1)] = following
        for place in reversed(range(pairs - 1)):
            row = row_of(place)
            following = (
                packed_inverse[chunk, row] * spectrum[row] + packed_factor[chunk, row] * following
            )
            upper_part[row] = following
        following = turn_plane(following)
        for place in reversed(range(pairs)):
            row = row_of(place)
            following = (
                packed_inverse[chunk, row] * spectrum[row] + packed_factor[chunk, row] * following
            )
            spectrum[row] = jnp.where(first_lanes, following, upper_part[row])
        edge_copy(1 + chunk).wait()
        edge = gain_here[chunk] * value + gain_there[chunk] * turn_plane(edge_in[1 + chunk])
        edge = jnp.where(first_lanes, turn_plane(edge), edge)
        for row in range(0, pairs, 2):
            first = spectrum[row] + packed_response[chunk, row] * edge
            second = spectrum[row + 1] + packed_response[chunk, row + 1] * edge
            value = transform_y(flat(first), flat(second))
            send_b[chunk, :, row] = value[:, :width].reshape(count, y_rows, width)
            send_b[chunk, :, row + 1] = value[:, width:].reshape(count, y_rows, width)
        for target in [4 * far + step for step in range(4)] + near_targets:
            send_back(chunk, target).start()
        recv_b[chunk, me] = send_b[chunk, me]

    for kind in (2, 3):
        for block in range(4):
            table_copy(kind, block).wait()

    def gathered(chunk, side):
        tops = []
        bottoms = []
        for pair in range(2):
            even = flat(recv_b[chunk, 4 * side + 2 * pair])
            odd = flat(recv_b[chunk, 4 * side + 2 * pair + 1])
            top, bottom = mix(even, odd)
            tops.append(top)
            bottoms.append(bottom)
        value = jnp.concatenate(
            [jnp.concatenate(tops, axis=1), jnp.concatenate(bottoms, axis=1)], axis=0
        )
        upper, lower = split_values(value)
        return jnp.concatenate([upper, lower], axis=0), upper

    def product(stacked, upper, block, columns):
        first = dot32(stacked, back_high_v[block, :, columns])
        return first[:rows] + first[rows:] + dot32(upper, back_low_v[block, :, columns])

    for step in range(4):
        chunk = step // 2
        side = near if step % 2 == 0 else far
        for source in near_targets if step % 2 == 0 else far_targets:
            wait_back(chunk, source)
        pieces = gathered(chunk, side)
        for index in range(count // 2):
            columns = slice(index * 2 * width, (index + 1) * 2 * width)
            total = product(*pieces, 2 * chunk + side, columns).reshape(layers, y_rows, 2 * width)
            if step > 0:
                total = total + result[:, :, columns]
            if step == 3:
                total = total * focus_v[:, :, columns]
            result[:, :, columns] = total

    for place, target in enumerate(others):
        if place > 2:
            send_forward(0, target).wait_send()
        send_forward(1, target).wait_send()
        send_back(0, target).wait_send()
        send_back(1, target).wait_send()


def kernel_body(residual, focus_bins, layer_class):
    layers, y_rows, x_cells = residual.shape
    count = lax.axis_size("hor")
    width = x_cells // count
    y_cells = y_rows * count
    forward = []
    backward = []
    for table in split_table(x_cells):
        table = table.reshape(x_cells, count, 2, width // 2).transpose(2, 1, 3, 0)
        table = np.ascontiguousarray(table.reshape(4, 2 * width, x_cells))
        backward.append(table)
        forward.append(np.ascontiguousarray(table.transpose(0, 2, 1)))
    high_y, low_y = split_table(y_cells)
    table_y = np.concatenate([high_y, low_y, high_y, low_y], axis=1)
    filler = np.broadcast_to(table_y, (4,) + table_y.shape)
    forward[0] = np.concatenate([forward[0], filler], axis=1)
    pairs = layers // 2
    block = (2, count, pairs, y_rows, width)
    plane = (y_cells // 8, 8, width)
    f32, bf16, dma = jnp.float32, jnp.bfloat16, pltpu.SemaphoreType.DMA
    return pl.pallas_call(
        kernel,
        out_shape=jax.ShapeDtypeStruct(residual.shape, f32),
        in_specs=[pl.BlockSpec(memory_space=pl.ANY)] * 7,
        out_specs=pl.BlockSpec(memory_space=pltpu.VMEM),
        scratch_shapes=[
            pltpu.VMEM(residual.shape, f32),
            pltpu.VMEM(residual.shape, jnp.int32),
            pltpu.SMEM((1, 2 * layers), jnp.int32),
            pltpu.VMEM(table_y.shape, bf16),
            pltpu.VMEM(forward[1].shape, bf16),
            pltpu.VMEM(forward[1].shape, bf16),
            pltpu.VMEM(backward[0].shape, bf16),
            pltpu.VMEM(backward[1].shape, bf16),
            pltpu.VMEM(residual.shape, f32),
            pltpu.VMEM(block, f32),
            pltpu.VMEM(block, f32),
            pltpu.VMEM(block, f32),
            pltpu.VMEM(block, f32),
            pltpu.VMEM((2 * layers, 8, width), f32),
            pltpu.VMEM((layers,) + plane, f32),
            pltpu.VMEM((layers,) + plane, f32),
            pltpu.VMEM((2, pairs) + plane, f32),
            pltpu.VMEM((2, pairs) + plane, f32),
            pltpu.VMEM((layers,) + plane, f32),
            pltpu.VMEM((2, pairs) + plane, f32),
            pltpu.VMEM((pairs,) + plane, f32),
            pltpu.VMEM((pairs,) + plane, f32),
            pltpu.VMEM((2,) + plane, f32),
            pltpu.VMEM((2,) + plane, f32),
            pltpu.VMEM((3,) + plane, f32),
            pltpu.VMEM((3,) + plane, f32),
            dma((4,)),
            dma((4, 4)),
            dma((2, count)),
            dma((2, count)),
            dma((2, count)),
            dma((2, count)),
            dma((3,)),
            dma((3,)),
        ],
        compiler_params=pltpu.CompilerParams(
            collective_id=0, has_side_effects=True, vmem_limit_bytes=54716 * 2**10
        ),
        cost_estimate=pl.CostEstimate(
            flops=2 * 6 * layers * y_rows * x_cells * x_cells,
            bytes_accessed=10 * 2**20,
            transcendentals=layers * y_rows * x_cells,
        ),
    )(
        residual,
        focus_bins,
        layer_class.reshape(1, -1),
        jnp.asarray(forward[0]),
        jnp.asarray(forward[1]),
        jnp.asarray(backward[0]),
        jnp.asarray(backward[1]),
    )


def fits_kernel(mesh):
    return mesh.shape["hor"] == 8 and mesh.shape["dep"] == 2


def chosen(mesh, residual, focus_bins, layer_class):
    shape = residual.shape
    if fits_kernel(mesh) and shape == (16, 8, 1024):
        return kernel_body(residual, focus_bins, layer_class)
    return body(residual, focus_bins, layer_class)


def solution(mesh):
    return jax.shard_map(
        functools.partial(chosen, mesh),
        mesh=mesh,
        in_specs=(P(("grp", "dep"), "hor", None), P(("grp", "dep"), "hor", None), P("grp")),
        out_specs=P(("grp", "dep"), "hor", None),
        check_vma=False,
    )
```
